256 devices in a mesh: grp: 16 (over z, core), ing: 16 (over y, x).
Axes of the slice: x: 4, y: 4, z: 8, core: 2. Of those that a mesh axis runs over, the one named last changes fastest.
Arguments:
- image_embed: bfloat16 [32768, 1152], P(('grp', 'ing')), may hold values from -20 to 20
- text_embed: bfloat16 [32768, 1152], P(('grp', 'ing')), may hold values from -20 to 20
- scale_logarithm: float32 [1], replicated, may hold values from 1.8 to 2.6
- logit_bias: float32 [1], replicated, may hold values from -4 to -1
- loss_grad: float32 [1], replicated, may hold values from 2048 to 8192
Outputs:
- image_gradient: float32 [32768, 1152], P(('grp', 'ing'))
- text_gradient: float32 [32768, 1152], P(('grp', 'ing'))
The draws below stay inside these ranges and needn't reach their ends.
All inputs are finite; a program needn't handle non-finite values.
Results may differ from the reference program's by a relative error of at most 0.0042.
Values may be sent and summed in bfloat16 or wider, within the bound.
No kernel may reach another device: no remote copies, remote signals or barrier semaphores. Data moves between devices by JAX's collectives and lax.ppermute only.
A program may use at most 128 MiB of HBM per device.

```python
import math
import jax
import jax.numpy as jnp
from jax import lax

EMBED_WIDTH = 1152
ROWS_DEV = 128
TOTAL_PAIRS = 32768
SET = 4096
N_ING = 16


def common_part(key):
    return jax.random.normal(key, (TOTAL_PAIRS, EMBED_WIDTH), jnp.float32)


def draw_image_embed(key, part):
    shared = common_part(key)
    key = jax.random.fold_in(key, 11)
    key_own, key_col, key_row = jax.random.split(key, 3)
    col_scale = jnp.exp(jax.random.uniform(key_col, (EMBED_WIDTH,), jnp.float32, 0.0, math.log(10.0)))
    row_scale = jnp.exp(jax.random.uniform(key_row, (TOTAL_PAIRS, 1), jnp.float32, 0.0, math.log(10.0)))
    own_part = jax.random.normal(key_own, (TOTAL_PAIRS, EMBED_WIDTH), jnp.float32)
    values = (0.6 * shared + 0.8 * own_part) * col_scale * row_scale
    values = jnp.clip(values / (3.0 * math.sqrt(EMBED_WIDTH)), -20.0, 20.0)
    return values.astype(jnp.bfloat16)


def draw_text_embed(key, part):
    shared = common_part(key)
    key = jax.random.fold_in(key, 23)
    key_own, key_col, key_row = jax.random.split(key, 3)
    col_scale = jnp.exp(jax.random.uniform(key_col, (EMBED_WIDTH,), jnp.float32, 0.0, math.log(10.0)))
    row_scale = jnp.exp(jax.random.uniform(key_row, (TOTAL_PAIRS, 1), jnp.float32, 0.0, math.log(10.0)))
    own_part = jax.random.normal(key_own, (TOTAL_PAIRS, EMBED_WIDTH), jnp.float32)
    values = (0.6 * shared + 0.8 * own_part) * col_scale * row_scale
    values = jnp.clip(values / (3.0 * math.sqrt(EMBED_WIDTH)), -20.0, 20.0)
    return values.astype(jnp.bfloat16)


def setup_inputs(seed: int = 0) -> dict:
    arg_keys = jax.random.split(jax.random.key(seed), 6)
    return {
        "image_embed": draw_image_embed(jax.random.fold_in(arg_keys[5], 71), 0),
        "text_embed": draw_text_embed(jax.random.fold_in(arg_keys[5], 71), 0),
        "scale_logarithm": jnp.clip(jax.random.uniform(arg_keys[2], (1,), jnp.float32, 1.8, 2.6), 1.8, 2.6),
        "logit_bias": jnp.clip(jax.random.uniform(arg_keys[3], (1,), jnp.float32, -4.0, -1.0), -4.0, -1.0),
        "loss_grad": jnp.clip(jnp.exp(jax.random.uniform(arg_keys[4], (1,), jnp.float32, math.log(2048.0), math.log(8192.0))), 2048.0, 8192.0),
    }


epsilon = 1e-06

def unit_rows(matrix):
    values = matrix.astype(jnp.float32)
    length = jnp.sqrt(lax.optimization_barrier(jnp.sum(values * values, axis=1, keepdims=True)) + epsilon)
    return (values / length, length)

def remove_projection(gradient, unit, length):
    return (gradient - unit * lax.optimization_barrier(jnp.sum(unit * gradient, axis=1, keepdims=True))) / length

def reference(image_embed, text_embed, scale_logarithm, logit_bias, loss_grad):
    image_unit_vector, image_length_norm = unit_rows(image_embed)
    text_unit_vector, text_length_norm = unit_rows(text_embed)
    image_halfway = image_unit_vector.astype(jnp.bfloat16)
    text_half = text_unit_vector.astype(jnp.bfloat16)
    softness_scale = jnp.exp(scale_logarithm[0])
    offset_bias = logit_bias[0]
    scale_factor = loss_grad[0] / SET
    block_len = ROWS_DEV * N_ING
    num_sets = TOTAL_PAIRS // SET
    image_sets = image_halfway.reshape(num_sets, SET, EMBED_WIDTH)
    text_sets = text_half.reshape(num_sets, SET, EMBED_WIDTH)

    def one_set(pair):
        image_set, text_set = pair
        image_blocks = image_set.reshape(2, block_len, EMBED_WIDTH)
        starts = jnp.arange(2, dtype=jnp.int32) * block_len
        col_ids = jnp.arange(SET, dtype=jnp.int32)[None, :]

        def scan_step(text_running, scan_in):
            image_blk, offset = scan_in
            cosine_scores = jnp.dot(image_blk, text_set.T, preferred_element_type=jnp.float32)
            logit_matrix = softness_scale * cosine_scores + offset_bias
            row_ids = offset + jnp.arange(block_len, dtype=jnp.int32)[:, None]
            labels = jnp.where(row_ids == col_ids, jnp.float32(1.0), jnp.float32(-1.0))
            weights = (-scale_factor * labels * jax.nn.sigmoid(-labels * logit_matrix)).astype(jnp.bfloat16)
            image_part = jnp.dot(weights, text_set, preferred_element_type=jnp.float32)
            text_running = text_running + jnp.dot(weights.T, image_blk, preferred_element_type=jnp.float32)
            return (text_running, image_part)
        text_running, image_pieces = lax.scan(scan_step, jnp.zeros((SET, EMBED_WIDTH), jnp.float32), (image_blocks, starts))
        return (image_pieces.reshape(SET, EMBED_WIDTH), text_running)
    image_pieces, text_pieces = lax.map(one_set, (image_sets, text_sets))
    image_direction = softness_scale * image_pieces.reshape(TOTAL_PAIRS, EMBED_WIDTH)
    text_direction = softness_scale * text_pieces.reshape(TOTAL_PAIRS, EMBED_WIDTH)
    return (remove_projection(image_direction, image_unit_vector, image_length_norm), remove_projection(text_direction, text_unit_vector, text_length_norm))
```

```python
import jax
import jax.numpy as jnp
from jax import lax
from jax.sharding import PartitionSpec as P

epsilon = 1e-06
AXES = ("grp", "ing")
SIDE = 4


def ring_pairs(step):
    pairs = []
    for grp in range(lax.axis_size("grp")):
        for ing in range(SIDE * SIDE):
            y, x = divmod(ing, SIDE)
            if grp % 2:
                y = (y + step) % SIDE
            else:
                x = (x + step) % SIDE
            pairs.append((grp * SIDE * SIDE + ing, grp * SIDE * SIDE + y * SIDE + x))
    return pairs


def hop(value, step):
    return lax.ppermute(value, AXES, ring_pairs(step))


def swap(value):
    size = SIDE * SIDE
    pairs = [
        (grp * size + ing, (grp ^ 1) * size + ing)
        for grp in range(lax.axis_size("grp"))
        for ing in range(size)
    ]
    return lax.ppermute(value, AXES, pairs)


def unit_rows(matrix):
    values = matrix.astype(jnp.float32)
    length = jnp.sqrt(jnp.sum(values * values, axis=1, keepdims=True) + epsilon)
    return (values / length, length)


def remove_projection(gradient, unit, length):
    return (gradient - unit * jnp.sum(unit * gradient, axis=1, keepdims=True)) / length


def logits_of(left, right, scale, bias):
    cosine = lax.dot_general(
        left, right, (((1,), (1,)), ((), ())), preferred_element_type=jnp.float32
    )
    return scale * cosine + bias


def body(image_embed, text_embed, scale_logarithm, logit_bias, loss_grad):
    rows = image_embed.shape[0]
    core = lax.axis_index("grp") % 2
    scale = jnp.exp(scale_logarithm[0])
    bias = logit_bias[0]
    factor = loss_grad[0] / (2 * rows * SIDE * SIDE)
    image_unit, image_length = unit_rows(image_embed)
    text_unit, text_length = unit_rows(text_embed)
    image_half = image_unit.astype(jnp.bfloat16)
    text_half = text_unit.astype(jnp.bfloat16)
    first = jnp.where(core == 0, image_half, text_half)
    other = jnp.where(core == 0, text_half, image_half)
    second = swap(other)

    back_first = hop(first, 1)
    ahead_second = hop(second, -1)
    back_second = hop(second, 1)
    ahead_first = hop(first, -1)
    far_first = hop(back_first, 1)
    far_second = hop(ahead_second, -1)

    own = jnp.concatenate([first, second], 0)
    back = jnp.concatenate([back_first, back_second], 0)
    ahead = jnp.concatenate([ahead_first, ahead_second], 0)
    far = jnp.concatenate([far_first, far_second], 0)
    other_own = swap(own)
    other_back = swap(back)
    other_ahead = swap(ahead)
    other_far = swap(far)

    def negative(left, right):
        return (factor * jax.nn.sigmoid(logits_of(left, right, scale, bias))).astype(jnp.bfloat16)

    def with_pairs(left, right):
        ids = jnp.arange(2 * rows, dtype=jnp.int32)
        same = ids[:, None] == ((ids + rows) % (2 * rows))[None, :]
        labels = jnp.where(same, jnp.float32(1.0), jnp.float32(-1.0))
        values = logits_of(left, right, scale, bias)
        return (-factor * labels * jax.nn.sigmoid(-labels * values)).astype(jnp.bfloat16)

    others = jnp.concatenate([other_own, other_back, other_ahead, other_far], 0)

    def share(left):
        return jnp.dot(negative(left, others), others, preferred_element_type=jnp.float32)

    share_far = share(far).astype(jnp.bfloat16)
    share_back = share(back)
    share_ahead = share(ahead)
    rest = jnp.concatenate([other_back, other_ahead, other_far], 0)
    share_own = jnp.dot(
        with_pairs(own, other_own), other_own, preferred_element_type=jnp.float32
    ) + jnp.dot(negative(own, rest), rest, preferred_element_type=jnp.float32)

    relay_first = hop(share_far[:rows], -1)
    relay_second = hop(share_far[rows:], 1)
    from_ahead_second = hop(share_back[rows:].astype(jnp.bfloat16), -1)
    from_back_first = hop(share_ahead[:rows].astype(jnp.bfloat16), 1)
    from_ahead_first = hop((share_back[:rows] + relay_first).astype(jnp.bfloat16), -1)
    from_back_second = hop((share_ahead[rows:] + relay_second).astype(jnp.bfloat16), 1)
    own_first = share_own[:rows] + from_back_first + from_ahead_first
    own_second = share_own[rows:] + from_back_second + from_ahead_second
    other_first = swap(own_second)
    image_dir = jnp.where(core == 0, own_first, other_first)
    text_dir = jnp.where(core == 0, other_first, own_first)
    image_gradient = remove_projection(scale * image_dir, image_unit, image_length)
    text_gradient = remove_projection(scale * text_dir, text_unit, text_length)
    return (image_gradient, text_gradient)


def solution(mesh):
    placed = (P(AXES, None), P(AXES, None), P(), P(), P())
    return jax.shard_map(
        body,
        mesh=mesh,
        in_specs=placed,
        out_specs=(P(AXES, None), P(AXES, None)),
        check_vma=False,
    )
```

```python
import jax
import jax.numpy as jnp
from jax import lax
from jax.experimental import pallas as pl
from jax.experimental.pallas import tpu as pltpu
from jax.sharding import PartitionSpec as P

epsilon = 1e-06
AXES = ("grp", "ing")
SIDE = 4
VMEM_BYTES = 16 * 1024 * 1024
VMEM = pl.BlockSpec(memory_space=pltpu.VMEM)
SMEM = pl.BlockSpec(memory_space=pltpu.SMEM)


def moved(value, step, core_change=0, ring_change=0):
    size = SIDE * SIDE
    pairs = []
    for grp in range(lax.axis_size("grp")):
        target = grp ^ core_change
        for ing in range(size):
            y, x = divmod(ing, SIDE)
            if (grp ^ ring_change) % 2:
                y = (y + step) % SIDE
            else:
                x = (x + step) % SIDE
            pairs.append((grp * size + ing, target * size + y * SIDE + x))
    return lax.ppermute(value, AXES, pairs)


def hop(value, step):
    return moved(value, step)


def cross(value, step):
    return moved(value, step, 1, 1)


def cross_back(value, step):
    return moved(value, step, 1, 0)


def swap(value):
    return moved(value, 0, 1)


def dot_t(left, right):
    return lax.dot_general(left, right, (((1,), (1,)), ((), ())), preferred_element_type=jnp.float32)


def dot(left, right):
    return jnp.dot(left, right, preferred_element_type=jnp.float32)


def call(kernel, outs, specs, flops, name):
    run = pl.pallas_call(
        kernel,
        out_shape=[pltpu.VMEM(o.shape, o.dtype) for o in outs],
        in_specs=specs,
        out_specs=[VMEM] * len(outs),
        cost_estimate=pl.CostEstimate(flops=flops, bytes_accessed=flops // 4000, transcendentals=0),
        compiler_params=pltpu.CompilerParams(vmem_limit_bytes=VMEM_BYTES),
        name=name,
    )
    return lambda *args: run(
        *[pltpu.with_memory_space_constraint(a, pltpu.VMEM) if s is VMEM else a for a, s in zip(args, specs)]
    )


def unit_rows(matrix):
    values = matrix.astype(jnp.float32)
    length = jnp.sqrt(jnp.sum(values * values, axis=1, keepdims=True) + epsilon)
    return (values / length, length)


def norm_kernel(core, image, text, first, other):
    image_half = unit_rows(image[...])[0].astype(jnp.bfloat16)
    text_half = unit_rows(text[...])[0].astype(jnp.bfloat16)

    @pl.when(core[0] == 0)
    def _():
        first[...] = image_half
        other[...] = text_half

    @pl.when(core[0] != 0)
    def _():
        first[...] = text_half
        other[...] = image_half


def negative(cosine, consts):
    return (consts[2] / (1.0 + jnp.exp(-(consts[0] * cosine + consts[1])))).astype(jnp.bfloat16)


def positive(cosine, consts):
    return (-consts[2] / (1.0 + jnp.exp(consts[0] * cosine + consts[1]))).astype(jnp.bfloat16)


def near_kernel(consts, first, other, second, other_second, back_first, back_second, ahead_first,
                ahead_second, near_others, late_others, w_own, w_back, w_ahead):
    rows = first.shape[0]
    lefts = [(w_own, first, second), (w_back, back_first, back_second), (w_ahead, ahead_first, ahead_second)]
    rights = [(other, other_second), (near_others,), (late_others,)]
    for place, parts in enumerate(rights):
        right = jnp.concatenate([p[...] for p in parts], 0) if len(parts) > 1 else parts[0][...]
        cols = pl.ds(place * 2 * rows, 2 * rows)
        for out, up, down in lefts:
            cosine = dot_t(jnp.concatenate([up[...], down[...]], 0), right)
            weights = negative(cosine, consts)
            if place == 0 and out is w_own:
                i = lax.broadcasted_iota(jnp.int32, cosine.shape, 0)
                j = lax.broadcasted_iota(jnp.int32, cosine.shape, 1)
                weights = jnp.where(i == j, positive(cosine, consts), weights)
            out[:, cols] = weights


def far_w_kernel(consts, far_first, far_second, other, other_second, near_others, late_others, w_far):
    rows = far_first.shape[0]
    left = jnp.concatenate([far_first[...], far_second[...]], 0)
    rights = [(other, other_second), (near_others,), (late_others,)]
    for place, parts in enumerate(rights):
        right = jnp.concatenate([p[...] for p in parts], 0) if len(parts) > 1 else parts[0][...]
        w_far[:, pl.ds(place * 2 * rows, 2 * rows)] = negative(dot_t(left, right), consts)


def mixed(weights, far_weights, other, other_second, near_others, late_others, far_others):
    rows = other.shape[0]
    total = dot(weights[:, : rows], other[...])
    total += dot(weights[:, rows : 2 * rows], other_second[...])
    total += dot(weights[:, 2 * rows : 4 * rows], near_others[...])
    total += dot(weights[:, 4 * rows :], late_others[...])
    return total + dot(far_weights, far_others[...])


def far_kernel(consts, w_far, far_first, far_second, other, other_second, near_others, late_others,
               far_others, share_first, share_second):
    rows = far_first.shape[0]
    left = jnp.concatenate([far_first[...], far_second[...]], 0)
    weights = negative(dot_t(left, far_others[...]), consts)
    total = mixed(w_far[...], weights, other, other_second, near_others, late_others, far_others)
    share_first[...] = total[:rows].astype(jnp.bfloat16)
    share_second[...] = total[rows:].astype(jnp.bfloat16)


def share_kernel(consts, w_back, w_ahead, back_first, back_second, ahead_first, ahead_second, other,
                 other_second, near_others, late_others, far_others, out_back_first, out_back_second,
                 out_ahead_first, out_ahead_second):
    rows = other.shape[0]
    for weights, up, down, out_up, out_down in (
        (w_back, back_first, back_second, out_back_first, out_back_second),
        (w_ahead, ahead_first, ahead_second, out_ahead_first, out_ahead_second),
    ):
        left = jnp.concatenate([up[...], down[...]], 0)
        last = negative(dot_t(left, far_others[...]), consts)
        total = mixed(weights[...], last, other, other_second, near_others, late_others, far_others)
        out_up[...] = total[:rows].astype(out_up.dtype)
        out_down[...] = total[rows:].astype(out_down.dtype)


def own_kernel(consts, w_own, first, second, other, other_second, near_others, late_others,
               far_others, out_first, out_second):
    rows = other.shape[0]
    left = jnp.concatenate([first[...], second[...]], 0)
    last = negative(dot_t(left, far_others[...]), consts)
    total = mixed(w_own[...], last, other, other_second, near_others, late_others, far_others)
    out_first[...] = total[:rows]
    out_second[...] = total[rows:]


def relay_kernel(up, up_got, down, down_got, up_out, down_out):
    up_out[...] = (up[...] + up_got[...].astype(jnp.float32)).astype(jnp.bfloat16)
    down_out[...] = (down[...] + down_got[...].astype(jnp.float32)).astype(jnp.bfloat16)


def last_kernel(core, consts, image, text, own, own_one, own_two, their, their_one, their_two, image_out, text_out):
    own_dir = consts[0] * (own[...] + own_one[...].astype(jnp.float32) + own_two[...].astype(jnp.float32))
    their_dir = consts[0] * (their[...] + their_one[...].astype(jnp.float32) + their_two[...].astype(jnp.float32))
    is_image = core[0] == 0
    for embed, out, direction in (
        (image, image_out, jnp.where(is_image, own_dir, their_dir)),
        (text, text_out, jnp.where(is_image, their_dir, own_dir)),
    ):
        unit, length = unit_rows(embed[...])
        out[...] = (direction - unit * jnp.sum(unit * direction, axis=1, keepdims=True)) / length


def body(image_embed, text_embed, scale_logarithm, logit_bias, loss_grad):
    rows, width = image_embed.shape
    half = jax.ShapeDtypeStruct((rows, width), jnp.bfloat16)
    full = jax.ShapeDtypeStruct((rows, width), jnp.float32)
    core = (lax.axis_index("grp") % 2).astype(jnp.int32).reshape(1)
    consts = jnp.concatenate(
        [jnp.exp(scale_logarithm), logit_bias, loss_grad / (2 * rows * SIDE * SIDE)]
    )
    unit = 2 * rows * rows * width

    first, other = call(norm_kernel, [half, half], [SMEM, VMEM, VMEM], 10**8, "norms")(
        core, image_embed, text_embed
    )
    back_first = hop(first, 1)
    ahead_second = cross(other, -1)
    other_second = swap(first)
    second = swap(other)
    back_second = hop(second, 1)
    ahead_first = cross(other_second, -1)
    near_others = swap(jnp.concatenate([back_first, ahead_second], 0))
    far_first = hop(back_first, 1)
    far_second = hop(ahead_second, -1)
    late_others = swap(jnp.concatenate([back_second, ahead_first], 0))
    far_others = swap(jnp.concatenate([far_first, far_second], 0))

    weights_shape = jax.ShapeDtypeStruct((2 * rows, 6 * rows), jnp.bfloat16)
    w_own, w_back, w_ahead = call(
        near_kernel, [weights_shape] * 3, [SMEM] + [VMEM] * 10, 36 * unit, "near"
    )(consts, first, other, second, other_second, back_first, back_second, ahead_first, ahead_second,
      near_others, late_others)
    (w_far,) = call(far_w_kernel, [weights_shape], [SMEM] + [VMEM] * 6, 12 * unit, "far_weights")(
        consts, far_first, far_second, other, other_second, near_others, late_others
    )
    others = (other, other_second, near_others, late_others, far_others)
    share_first, share_second = call(
        far_kernel, [half, half], [SMEM] + [VMEM] * 8, 20 * unit, "far"
    )(consts, w_far, far_first, far_second, *others)
    relay_first = hop(share_first, -1)
    relay_second = hop(share_second, 1)
    keep_back_first, share_back_second, share_ahead_first, keep_ahead_second = call(
        share_kernel, [full, half, half, full], [SMEM] + [VMEM] * 11, 40 * unit, "shares"
    )(consts, w_back, w_ahead, back_first, back_second, ahead_first, ahead_second, *others)
    their_one = cross_back(share_back_second, -1)
    own_one = hop(share_ahead_first, 1)
    own_first, own_second = call(own_kernel, [full, full], [SMEM] + [VMEM] * 8, 20 * unit, "own")(
        consts, w_own, first, second, *others
    )
    their_second = swap(own_second)
    send_first, send_second = call(relay_kernel, [half, half], [VMEM] * 4, 10**7, "relay")(
        keep_back_first, relay_first, keep_ahead_second, relay_second
    )
    own_two = hop(send_first, -1)
    their_two = cross_back(send_second, 1)
    image_gradient, text_gradient = call(
        last_kernel, [full, full], [SMEM] * 2 + [VMEM] * 8, 10**8, "last"
    )(core, consts, image_embed, text_embed, own_first, own_one, own_two, their_second, their_one, their_two)
    return (image_gradient, text_gradient)


def solution(mesh):
    placed = (P(AXES, None), P(AXES, None), P(), P(), P())
    return jax.shard_map(
        body,
        mesh=mesh,
        in_specs=placed,
        out_specs=(P(AXES, None), P(AXES, None)),
        check_vma=False,
    )
```

```python
import math

import jax
import jax.numpy as jnp
from jax import lax
from jax.experimental import pallas as pl
from jax.experimental.pallas import tpu as pltpu
from jax.sharding import PartitionSpec as P

epsilon = 1e-06
AXES = ("grp", "ing")
SIDE = 4
VMEM_BYTES = 16 * 1024 * 1024
VMEM = pl.BlockSpec(memory_space=pltpu.VMEM)
SMEM = pl.BlockSpec(memory_space=pltpu.SMEM)
HBM = pl.BlockSpec(memory_space=pl.ANY)


def moved(value, step, core_change=0, ring_change=0):
    size = SIDE * SIDE
    pairs = []
    for grp in range(lax.axis_size("grp")):
        target = grp ^ core_change
        for ing in range(size):
            y, x = divmod(ing, SIDE)
            if (grp ^ ring_change) % 2:
                y = (y + step) % SIDE
            else:
                x = (x + step) % SIDE
            pairs.append((grp * size + ing, target * size + y * SIDE + x))
    return lax.ppermute(value, AXES, pairs)


def hop(value, step):
    return moved(value, step)


def cross(value, step):
    return moved(value, step, 1, 1)


def cross_back(value, step):
    return moved(value, step, 1, 0)


def swap(value):
    return moved(value, 0, 1)


def dot_t(left, right):
    return lax.dot_general(left, right, (((1,), (1,)), ((), ())), preferred_element_type=jnp.float32)


def dot(left, right):
    return jnp.dot(left, right, preferred_element_type=jnp.float32)


def call(kernel, outs, specs, flops, name, out_specs=None, scratch=()):
    out_specs = out_specs or [VMEM] * len(outs)
    run = pl.pallas_call(
        kernel,
        out_shape=[pltpu.VMEM(o.shape, o.dtype) if s is VMEM else o for o, s in zip(outs, out_specs)],
        in_specs=specs,
        out_specs=out_specs,
        scratch_shapes=scratch,
        cost_estimate=pl.CostEstimate(flops=flops, bytes_accessed=1, transcendentals=0),
        compiler_params=pltpu.CompilerParams(vmem_limit_bytes=VMEM_BYTES),
        name=name,
    )
    return lambda *args: run(
        *[
            pltpu.with_memory_space_constraint(a, pltpu.VMEM if s is VMEM else pltpu.HBM) if s is not SMEM else a
            for a, s in zip(args, specs)
        ]
    )


def unit_rows(matrix):
    values = matrix.astype(jnp.float32)
    length = jnp.sqrt(jnp.sum(values * values, axis=1, keepdims=True) + epsilon)
    return (values / length, length)


def rows_kernel(core, image, text, first, other, raw_first, raw_other, sems):

    @pl.when(core[0] == 0)
    def _():
        pltpu.make_async_copy(image, raw_first, sems.at[0]).start()
        pltpu.make_async_copy(text, raw_other, sems.at[1]).start()

    @pl.when(core[0] != 0)
    def _():
        pltpu.make_async_copy(text, raw_first, sems.at[0]).start()
        pltpu.make_async_copy(image, raw_other, sems.at[1]).start()

    pltpu.make_async_copy(image, raw_first, sems.at[0]).wait()
    first[...] = unit_rows(raw_first[...])[0].astype(jnp.bfloat16)
    pltpu.make_async_copy(text, raw_other, sems.at[1]).wait()
    other[...] = unit_rows(raw_other[...])[0].astype(jnp.bfloat16)


def consts_kernel(numbers, after, consts):
    scale = jnp.exp(numbers[0:8])
    consts[0:8] = scale
    consts[8:16] = scale * (-math.log2(math.e))
    consts[16:24] = numbers[8:16] * (-math.log2(math.e))
    consts[24:32] = numbers[16:24] / (2 * after.shape[0] * SIDE * SIDE)


def negative(cosine, consts):
    power = cosine * consts[8:9, 0:1] + consts[16:17, 0:1]
    return (consts[24:25, 0:1] / (1.0 + jnp.exp2(power))).astype(jnp.bfloat16)


def positive(cosine, consts):
    power = cosine * consts[8:9, 0:1] + consts[16:17, 0:1]
    return (-consts[24:25, 0:1] / (1.0 + jnp.exp2(-power))).astype(jnp.bfloat16)


def joined(up, down):
    return jnp.concatenate([up[...], down[...]], 0)


def near_kernel(consts, first, second, back_first, ahead_second, other, other_second, near_others, part_own,
                part_back_first, part_ahead_second):
    rows = first.shape[0]
    left = jnp.concatenate([first[...], second[...], back_first[...], ahead_second[...]], 0)
    right = joined(other, other_second)
    cosine = dot_t(left, right)
    weights = negative(cosine, consts)
    pairs = cosine[: 2 * rows]
    i = lax.broadcasted_iota(jnp.int32, pairs.shape, 0)
    j = lax.broadcasted_iota(jnp.int32, pairs.shape, 1)
    own = jnp.where(i == j, positive(pairs, consts), weights[: 2 * rows])
    total = dot(jnp.concatenate([own, weights[2 * rows :]], 0), right)
    total += dot(negative(dot_t(left, near_others[...]), consts), near_others[...])
    part_own[...] = total[: 2 * rows]
    part_back_first[...] = total[2 * rows : 3 * rows]
    part_ahead_second[...] = total[3 * rows :]


def second_kernel(consts, back_second, ahead_first, other, other_second, near_others, part_back_second,
                  part_ahead_first):
    rows = back_second.shape[0]
    left = joined(back_second, ahead_first)
    right = joined(other, other_second)
    total = dot(negative(dot_t(left, right), consts), right)
    total += dot(negative(dot_t(left, near_others[...]), consts), near_others[...])
    part_back_second[...] = total[:rows]
    part_ahead_first[...] = total[rows:]


def far_near_kernel(consts, far_first, far_second, other, other_second, near_others, late_others, part):
    left = joined(far_first, far_second)
    right = joined(other, other_second)
    total = dot(negative(dot_t(left, right), consts), right)
    for others in (near_others, late_others):
        total += dot(negative(dot_t(left, others[...]), consts), others[...])
    part[...] = total


def far_kernel(consts, part, far_first, far_second, far_others_first, far_others_second, share_first, share_second):
    rows = far_first.shape[0]
    others = joined(far_others_first, far_others_second)
    weights = negative(dot_t(joined(far_first, far_second), others), consts)
    total = part[...] + dot(weights, others)
    share_first[...] = total[:rows].astype(jnp.bfloat16)
    share_second[...] = total[rows:].astype(jnp.bfloat16)


def rest_kernel(consts, part_own, part_back_first, part_back_second, part_ahead_first, part_ahead_second, first, second,
                back_first, back_second, ahead_first, ahead_second, late_others, far_others_first, far_others_second,
                after, own_first, own_second, out_back_first, out_back_second, out_ahead_first, out_ahead_second):
    rows = first.shape[0]
    late = late_others[...]
    far_others = joined(far_others_first, far_others_second)
    for up, down, part, out_up, out_down in (
        (back_first, back_second, (part_back_first, part_back_second), out_back_first, out_back_second),
        (ahead_first, ahead_second, (part_ahead_first, part_ahead_second), out_ahead_first, out_ahead_second),
        (first, second, (part_own,), own_first, own_second),
    ):
        left = joined(up, down)
        total = dot(negative(dot_t(left, late), consts), late)
        total += dot(negative(dot_t(left, far_others), consts), far_others)
        total += joined(*part) if len(part) > 1 else part[0][...]
        out_up[...] = total[:rows].astype(out_up.dtype)
        out_down[...] = total[rows:].astype(out_down.dtype)


def relay_kernel(up, up_got, down, down_got, up_out, down_out):
    up_out[...] = (up[...] + up_got[...].astype(jnp.float32)).astype(jnp.bfloat16)
    down_out[...] = (down[...] + down_got[...].astype(jnp.float32)).astype(jnp.bfloat16)


def last_kernel(core, consts, raw_first, raw_other, own, own_one, own_two, their, their_one, their_two,
                image_out, text_out, own_grad, their_grad, sems):
    rows = own.shape[0]
    parts = sems.shape[1]
    block = rows // parts
    scale = consts[0:1, 0:1]
    for part in range(parts):
        at = pl.ds(part * block, block)
        for kind, (raw, mine, one, two, grad) in enumerate((
            (raw_first, own, own_one, own_two, own_grad),
            (raw_other, their, their_one, their_two, their_grad),
        )):
            direction = scale * (mine[at] + one[at].astype(jnp.float32) + two[at].astype(jnp.float32))
            unit, length = unit_rows(raw[at])
            grad[at] = (direction - unit * jnp.sum(unit * direction, axis=1, keepdims=True)) / length
            sem = sems.at[kind, part]
            for value, out in ((0, (image_out, text_out)[kind]), (1, (text_out, image_out)[kind])):

                @pl.when(core[0] == value)
                def _(grad=grad, out=out, at=at, sem=sem):
                    pltpu.make_async_copy(grad.at[at], out.at[at], sem).start()

    for part in range(parts):
        at = pl.ds(part * block, block)
        pltpu.make_async_copy(own_grad.at[at], image_out.at[at], sems.at[0, part]).wait()
        pltpu.make_async_copy(their_grad.at[at], text_out.at[at], sems.at[1, part]).wait()


def gate_kernel(value, after, out):
    pass


def gate(value, after):
    return pl.pallas_call(
        gate_kernel,
        out_shape=pltpu.VMEM(value.shape, value.dtype),
        in_specs=[VMEM, VMEM],
        out_specs=VMEM,
        input_output_aliases={0: 0},
        cost_estimate=pl.CostEstimate(flops=1, bytes_accessed=1, transcendentals=0),
        compiler_params=pltpu.CompilerParams(vmem_limit_bytes=VMEM_BYTES),
        name="gate",
    )(pltpu.with_memory_space_constraint(value, pltpu.VMEM), pltpu.with_memory_space_constraint(after, pltpu.VMEM))


def pair_kernel(up, down, after, out):
    rows = up.shape[0]
    out[:rows] = up[...]
    out[rows:] = down[...]


def body(image_embed, text_embed, scale_logarithm, logit_bias, loss_grad):
    rows, width = image_embed.shape
    half = jax.ShapeDtypeStruct((rows, width), jnp.bfloat16)
    full = jax.ShapeDtypeStruct((rows, width), jnp.float32)
    double = jax.ShapeDtypeStruct((2 * rows, width), jnp.float32)
    core = (lax.axis_index("grp") % 2).astype(jnp.int32).reshape(1)
    numbers = jnp.concatenate(
        [jnp.broadcast_to(value, (8, 128)) for value in (scale_logarithm, logit_bias, loss_grad)], 0
    )
    unit = 2 * rows * rows * width

    first, other, raw_first, raw_other = call(
        rows_kernel,
        [half, half, half, half],
        [SMEM, HBM, HBM],
        10**8,
        "rows",
        scratch=[pltpu.SemaphoreType.DMA((2,))],
    )(core, image_embed, text_embed)

    back_first = hop(first, 1)
    ahead_second = cross(other, -1)
    other_second = swap(first)
    second = swap(other)
    (consts,) = call(consts_kernel, [jax.ShapeDtypeStruct((32, 128), jnp.float32)], [VMEM] * 2, 1, "consts")(
        numbers, second
    )
    back_second = hop(second, 1)
    ahead_first = cross(other_second, -1)
    far_first = hop(back_first, 1)
    far_second = hop(ahead_second, -1)
    (near,) = call(pair_kernel, [jax.ShapeDtypeStruct((2 * rows, width), jnp.bfloat16)], [VMEM] * 3, 1, "pair")(
        back_first, ahead_second, consts
    )
    near_others = swap(near)
    late_others = swap(jnp.concatenate([back_second, ahead_first], 0))
    part_own, part_back_first, part_ahead_second = call(near_kernel, [double, full, full], [VMEM] * 8, 1, "near")(
        consts, first, second, back_first, ahead_second, other, other_second, near_others
    )
    part_back_second, part_ahead_first = call(second_kernel, [full] * 2, [VMEM] * 6, 1, "second")(
        consts, back_second, ahead_first, other, other_second, near_others
    )
    far_first = gate(far_first, part_back_second)
    far_second = gate(far_second, part_own)
    far_others_first = swap(far_first)
    far_others_second = swap(far_second)
    (part_far,) = call(far_near_kernel, [double], [VMEM] * 7, 1, "far_near")(
        consts, far_first, far_second, other, other_second, near_others, late_others
    )
    share_first, share_second = call(far_kernel, [half, half], [VMEM] * 6, 8 * unit, "far")(
        consts, part_far, far_first, far_second, far_others_first, far_others_second
    )

    relay_first = hop(share_first, -1)
    relay_second = hop(share_second, 1)
    own_first, own_second, keep_back_first, share_back_second, share_ahead_first, keep_ahead_second = call(
        rest_kernel, [full, full, full, half, half, full], [VMEM] * 16, 40 * unit, "rest"
    )(
        consts, part_own, part_back_first, part_back_second, part_ahead_first, part_ahead_second, first, second,
        back_first, back_second, ahead_first, ahead_second, late_others, far_others_first, far_others_second, share_first,
    )
    their_one = cross_back(share_back_second, -1)
    own_one = hop(share_ahead_first, 1)
    their_second = swap(own_second)
    send_first, send_second = call(relay_kernel, [half, half], [VMEM] * 4, 10**7, "relay")(
        keep_back_first, relay_first, keep_ahead_second, relay_second
    )
    own_two = hop(send_first, -1)
    their_two = cross_back(send_second, 1)
    image_gradient, text_gradient = call(
        last_kernel,
        [full, full],
        [SMEM] + [VMEM] * 9,
        10**8,
        "last",
        out_specs=[HBM] * 2,
        scratch=[
            pltpu.VMEM((rows, width), jnp.float32),
            pltpu.VMEM((rows, width), jnp.float32),
            pltpu.SemaphoreType.DMA((2, 4)),
        ],
    )(core, consts, raw_first, raw_other, own_first, own_one, own_two, their_second, their_one, their_two)
    return (image_gradient, text_gradient)


def solution(mesh):
    placed = (P(AXES, None), P(AXES, None), P(), P(), P())
    return jax.shard_map(
        body,
        mesh=mesh,
        in_specs=placed,
        out_specs=(P(AXES, None), P(AXES, None)),
        check_vma=False,
    )
```

```python
import math

import jax
import jax.numpy as jnp
from jax import lax
from jax.experimental import pallas as pl
from jax.experimental.pallas import tpu as pltpu
from jax.sharding import PartitionSpec as P

epsilon = 1e-06
AXES = ("grp", "ing")
SIDE = 4
C1 = 1
C2 = 1
C3 = 1
C4 = 1
VMEM_BYTES = 16 * 1024 * 1024
VMEM = pl.BlockSpec(memory_space=pltpu.VMEM)
SMEM = pl.BlockSpec(memory_space=pltpu.SMEM)
HBM = pl.BlockSpec(memory_space=pl.ANY)


def moved(value, step, core_change=0, ring_change=0):
    size = SIDE * SIDE
    pairs = []
    for grp in range(lax.axis_size("grp")):
        target = grp ^ core_change
        for ing in range(size):
            y, x = divmod(ing, SIDE)
            if (grp ^ ring_change) % 2:
                y = (y + step) % SIDE
            else:
                x = (x + step) % SIDE
            pairs.append((grp * size + ing, target * size + y * SIDE + x))
    return lax.ppermute(value, AXES, pairs)


def hop(value, step):
    return moved(value, step)


def cross(value, step):
    return moved(value, step, 1, 1)


def cross_back(value, step):
    return moved(value, step, 1, 0)


def swap(value):
    return moved(value, 0, 1)


def dot_t(left, right):
    return lax.dot_general(left, right, (((1,), (1,)), ((), ())), preferred_element_type=jnp.float32)


def dot(left, right):
    return jnp.dot(left, right, preferred_element_type=jnp.float32)


def call(kernel, outs, specs, flops, name, out_specs=None, scratch=()):
    out_specs = out_specs or [VMEM] * len(outs)
    run = pl.pallas_call(
        kernel,
        out_shape=[pltpu.VMEM(o.shape, o.dtype) if s is VMEM else o for o, s in zip(outs, out_specs)],
        in_specs=specs,
        out_specs=out_specs,
        scratch_shapes=scratch,
        cost_estimate=pl.CostEstimate(flops=flops, bytes_accessed=1, transcendentals=0),
        compiler_params=pltpu.CompilerParams(vmem_limit_bytes=VMEM_BYTES),
        name=name,
    )
    return lambda *args: run(
        *[
            pltpu.with_memory_space_constraint(a, pltpu.VMEM if s is VMEM else pltpu.HBM) if s is not SMEM else a
            for a, s in zip(args, specs)
        ]
    )


def unit_rows(matrix):
    values = matrix.astype(jnp.float32)
    length = jnp.sqrt(jnp.sum(values * values, axis=1, keepdims=True) + epsilon)
    return (values / length, length)


def rows_kernel(core, image, text, first, other, raw_first, raw_other, sems):

    @pl.when(core[0] == 0)
    def _():
        pltpu.make_async_copy(image, raw_first, sems.at[0]).start()
        pltpu.make_async_copy(text, raw_other, sems.at[1]).start()

    @pl.when(core[0] != 0)
    def _():
        pltpu.make_async_copy(text, raw_first, sems.at[0]).start()
        pltpu.make_async_copy(image, raw_other, sems.at[1]).start()

    pltpu.make_async_copy(image, raw_first, sems.at[0]).wait()
    first[...] = unit_rows(raw_first[...])[0].astype(jnp.bfloat16)
    pltpu.make_async_copy(text, raw_other, sems.at[1]).wait()
    other[...] = unit_rows(raw_other[...])[0].astype(jnp.bfloat16)


def consts_kernel(numbers, after, after_too, consts):
    scale = jnp.exp(numbers[0:8])
    consts[0:8] = scale
    consts[8:16] = scale * (-math.log2(math.e))
    consts[16:24] = numbers[8:16] * (-math.log2(math.e))
    consts[24:32] = numbers[16:24] / (2 * after.shape[0] * SIDE * SIDE)


def negative(cosine, consts):
    power = cosine * consts[8:9, 0:1] + consts[16:17, 0:1]
    return (consts[24:25, 0:1] / (1.0 + jnp.exp2(power))).astype(jnp.bfloat16)


def positive(cosine, consts):
    power = cosine * consts[8:9, 0:1] + consts[16:17, 0:1]
    return (-consts[24:25, 0:1] / (1.0 + jnp.exp2(-power))).astype(jnp.bfloat16)


def joined(up, down):
    return jnp.concatenate([up[...], down[...]], 0)


def near_kernel(consts, back_first, back_second, ahead_first, ahead_second, other, other_second, near_first,
                near_second, part_back, part_ahead):
    rows = back_first.shape[0]
    left = jnp.concatenate([back_first[...], back_second[...], ahead_first[...], ahead_second[...]], 0)
    right = joined(other, other_second)
    total = dot(negative(dot_t(left, right), consts), right)
    right = joined(near_first, near_second)
    total += dot(negative(dot_t(left, right), consts), right)
    part_back[...] = total[: 2 * rows]
    part_ahead[...] = total[2 * rows :]


def far_near_kernel(consts, far_first, far_second, other, other_second, near_first, near_second, late_others, part):
    left = joined(far_first, far_second)
    right = joined(other, other_second)
    total = dot(negative(dot_t(left, right), consts), right)
    for right in (joined(near_first, near_second), late_others[...]):
        total += dot(negative(dot_t(left, right), consts), right)
    part[...] = total


def far_kernel(consts, part, far_first, far_second, far_others_first, far_others_second, share_first, share_second):
    rows = far_first.shape[0]
    others = joined(far_others_first, far_others_second)
    weights = negative(dot_t(joined(far_first, far_second), others), consts)
    total = part[...] + dot(weights, others)
    share_first[...] = total[:rows].astype(jnp.bfloat16)
    share_second[...] = total[rows:].astype(jnp.bfloat16)


def rest_kernel(consts, part_back, part_ahead, back_first, back_second, ahead_first, ahead_second, late_others,
                far_others_first, far_others_second, after, keep_back_first, share_back_second, share_ahead_first,
                keep_ahead_second):
    rows = back_first.shape[0]
    late = late_others[...]
    far_others = joined(far_others_first, far_others_second)
    left = jnp.concatenate([back_first[...], back_second[...], ahead_first[...], ahead_second[...]], 0)
    total = dot(negative(dot_t(left, late), consts), late)
    total += dot(negative(dot_t(left, far_others), consts), far_others)
    keep_back_first[...] = total[:rows] + part_back[:rows]
    share_back_second[...] = (total[rows : 2 * rows] + part_back[rows:]).astype(jnp.bfloat16)
    share_ahead_first[...] = (total[2 * rows : 3 * rows] + part_ahead[:rows]).astype(jnp.bfloat16)
    keep_ahead_second[...] = total[3 * rows :] + part_ahead[rows:]


def units_kernel(raw_first, raw_other, after, unit_own, length_own, unit_their, length_their):
    unit_own[...], length_own[...] = unit_rows(raw_first[...])
    unit_their[...], length_their[...] = unit_rows(raw_other[...])


def own_kernel(consts, first, second, back_first, back_second, ahead_first, ahead_second, far_first, far_second, other,
               other_second, near_first, near_second, late_others, far_others_first, far_others_second, after, own,
               their):
    for left, pairs, rights, out in (
        (first, joined(other, other_second),
         [joined(near_first, near_second), late_others[...], joined(far_others_first, far_others_second)], own),
        (other, joined(first, second),
         [joined(back_first, back_second), joined(ahead_first, ahead_second), joined(far_first, far_second)], their),
    ):
        cosine = dot_t(left[...], pairs)
        i = lax.broadcasted_iota(jnp.int32, cosine.shape, 0)
        j = lax.broadcasted_iota(jnp.int32, cosine.shape, 1)
        weights = jnp.where(i == j, positive(cosine, consts), negative(cosine, consts))
        total = dot(weights, pairs)
        for right in rights:
            total += dot(negative(dot_t(left[...], right), consts), right)
        out[...] = total


def relay_kernel(up, up_got, down, down_got, up_out, down_out):
    up_out[...] = (up[...] + up_got[...].astype(jnp.float32)).astype(jnp.bfloat16)
    down_out[...] = (down[...] + down_got[...].astype(jnp.float32)).astype(jnp.bfloat16)


def last_kernel(core, consts, unit_own, length_own, unit_their, length_their, own, own_one, own_two, their, their_one,
                their_two, image_out, text_out, own_grad, their_grad, sems):
    rows = own.shape[0]
    parts = sems.shape[1]
    block = rows // parts
    scale = consts[0:1, 0:1]
    for part in range(parts):
        at = pl.ds(part * block, block)
        for kind, (units, length, mine, one, two, grad) in enumerate((
            (unit_own, length_own, own, own_one, own_two, own_grad),
            (unit_their, length_their, their, their_one, their_two, their_grad),
        )):
            direction = scale * (mine[at] + one[at].astype(jnp.float32) + two[at].astype(jnp.float32))
            unit = units[at]
            grad[at] = (direction - unit * jnp.sum(unit * direction, axis=1, keepdims=True)) / length[at]
            sem = sems.at[kind, part]
            for value, out in ((0, (image_out, text_out)[kind]), (1, (text_out, image_out)[kind])):

                @pl.when(core[0] == value)
                def _(grad=grad, out=out, at=at, sem=sem):
                    pltpu.make_async_copy(grad.at[at], out.at[at], sem).start()

    for part in range(parts):
        at = pl.ds(part * block, block)
        pltpu.make_async_copy(own_grad.at[at], image_out.at[at], sems.at[0, part]).wait()
        pltpu.make_async_copy(their_grad.at[at], text_out.at[at], sems.at[1, part]).wait()


def gate_kernel(value, after, out):
    pass


def gate(value, after):
    return pl.pallas_call(
        gate_kernel,
        out_shape=pltpu.VMEM(value.shape, value.dtype),
        in_specs=[VMEM, VMEM],
        out_specs=VMEM,
        input_output_aliases={0: 0},
        cost_estimate=pl.CostEstimate(flops=1, bytes_accessed=1, transcendentals=0),
        compiler_params=pltpu.CompilerParams(vmem_limit_bytes=VMEM_BYTES),
        name="gate",
    )(pltpu.with_memory_space_constraint(value, pltpu.VMEM), pltpu.with_memory_space_constraint(after, pltpu.VMEM))


def body(image_embed, text_embed, scale_logarithm, logit_bias, loss_grad):
    rows, width = image_embed.shape
    half = jax.ShapeDtypeStruct((rows, width), jnp.bfloat16)
    full = jax.ShapeDtypeStruct((rows, width), jnp.float32)
    double = jax.ShapeDtypeStruct((2 * rows, width), jnp.float32)
    core = (lax.axis_index("grp") % 2).astype(jnp.int32).reshape(1)
    numbers = jnp.concatenate(
        [jnp.broadcast_to(value, (8, 128)) for value in (scale_logarithm, logit_bias, loss_grad)], 0
    )
    unit = 2 * rows * rows * width

    first, other, raw_first, raw_other = call(
        rows_kernel,
        [half, half, half, half],
        [SMEM, HBM, HBM],
        10**8,
        "rows",
        scratch=[pltpu.SemaphoreType.DMA((2,))],
    )(core, image_embed, text_embed)

    back_first = hop(first, 1)
    ahead_second = cross(other, -1)
    other_second = swap(first)
    second = swap(other)
    (consts,) = call(consts_kernel, [jax.ShapeDtypeStruct((32, 128), jnp.float32)], [VMEM] * 3, 1, "consts")(
        numbers, second, other_second
    )
    back_second = hop(second, 1)
    ahead_first = cross(other_second, -1)
    back_first = gate(back_first, consts)
    ahead_second = gate(ahead_second, consts)
    far_first = hop(back_first, 1)
    far_second = hop(ahead_second, -1)
    near_others = (swap(back_first), swap(ahead_second))
    backs = (back_first, back_second)
    aheads = (ahead_first, ahead_second)
    late_others = swap(jnp.concatenate([back_second, ahead_first], 0))
    part_back, part_ahead = call(near_kernel, [double] * 2, [VMEM] * 9, 1, "near")(
        consts, *backs, *aheads, other, other_second, *near_others
    )
    column = jax.ShapeDtypeStruct((rows, 1), jnp.float32)
    units = call(units_kernel, [full, column, full, column], [VMEM] * 3, 1, "units")(raw_first, raw_other, part_back)
    far_first = gate(far_first, part_back)
    far_second = gate(far_second, units[0])
    far_others_first = swap(far_first)
    far_others_second = swap(far_second)
    (part_far,) = call(far_near_kernel, [double], [VMEM] * 8, 1, "far_near")(
        consts, far_first, far_second, other, other_second, *near_others, late_others
    )
    share_first, share_second = call(far_kernel, [half, half], [VMEM] * 6, 8 * unit, "far")(
        consts, part_far, far_first, far_second, far_others_first, far_others_second
    )

    relay_first = hop(share_first, -1)
    relay_second = hop(share_second, 1)
    far_others = (far_others_first, far_others_second)
    keep_back_first, share_back_second, share_ahead_first, keep_ahead_second = call(
        rest_kernel, [full, half, half, full], [VMEM] * 11, C1, "rest"
    )(consts, part_back, part_ahead, *backs, *aheads, late_others, *far_others, share_first)
    their_one = cross_back(share_back_second, -1)
    own_one = hop(share_ahead_first, 1)
    send_first, send_second = call(relay_kernel, [half, half], [VMEM] * 4, C3, "relay")(
        keep_back_first, relay_first, keep_ahead_second, relay_second
    )
    own_two = hop(send_first, -1)
    their_two = cross_back(send_second, 1)
    own, their = call(own_kernel, [full, full], [VMEM] * 17, C2, "own")(
        consts, first, second, *backs, *aheads, far_first, far_second, other, other_second, *near_others, late_others,
        *far_others, send_first,
    )
    image_gradient, text_gradient = call(
        last_kernel,
        [full, full],
        [SMEM] + [VMEM] * 11,
        C4,
        "last",
        out_specs=[HBM] * 2,
        scratch=[
            pltpu.VMEM((rows, width), jnp.float32),
            pltpu.VMEM((rows, width), jnp.float32),
            pltpu.SemaphoreType.DMA((2, 4)),
        ],
    )(core, consts, *units, own, own_one, own_two, their, their_one, their_two)
    return (image_gradient, text_gradient)


def solution(mesh):
    placed = (P(AXES, None), P(AXES, None), P(), P(), P())
    return jax.shard_map(
        body,
        mesh=mesh,
        in_specs=placed,
        out_specs=(P(AXES, None), P(AXES, None)),
        check_vma=False,
    )
```

```python
import math

import jax
import jax.numpy as jnp
from jax import lax
from jax.experimental import pallas as pl
from jax.experimental.pallas import tpu as pltpu
from jax.sharding import PartitionSpec as P

epsilon = 1e-06
AXES = ("grp", "ing")
SIDE = 4
C1 = 1
C2 = 1
C3 = 1
C4 = 1
VMEM_BYTES = 16 * 1024 * 1024
VMEM = pl.BlockSpec(memory_space=pltpu.VMEM)
SMEM = pl.BlockSpec(memory_space=pltpu.SMEM)
HBM = pl.BlockSpec(memory_space=pl.ANY)


def moved(value, step, core_change=0, ring_change=0):
    size = SIDE * SIDE
    pairs = []
    for grp in range(lax.axis_size("grp")):
        target = grp ^ core_change
        for ing in range(size):
            y, x = divmod(ing, SIDE)
            if (grp ^ ring_change) % 2:
                y = (y + step) % SIDE
            else:
                x = (x + step) % SIDE
            pairs.append((grp * size + ing, target * size + y * SIDE + x))
    return lax.ppermute(value, AXES, pairs)


def hop(value, step):
    return moved(value, step)


def cross(value, step):
    return moved(value, step, 1, 1)


def cross_back(value, step):
    return moved(value, step, 1, 0)


def swap(value):
    return moved(value, 0, 1)


def dot_t(left, right):
    return lax.dot_general(left, right, (((1,), (1,)), ((), ())), preferred_element_type=jnp.float32)


def dot(left, right):
    return jnp.dot(left, right, preferred_element_type=jnp.float32)


def call(kernel, outs, specs, flops, name, out_specs=None, scratch=()):
    out_specs = out_specs or [VMEM] * len(outs)
    run = pl.pallas_call(
        kernel,
        out_shape=[pltpu.VMEM(o.shape, o.dtype) if s is VMEM else o for o, s in zip(outs, out_specs)],
        in_specs=specs,
        out_specs=out_specs,
        scratch_shapes=scratch,
        cost_estimate=pl.CostEstimate(flops=flops, bytes_accessed=1, transcendentals=0),
        compiler_params=pltpu.CompilerParams(vmem_limit_bytes=VMEM_BYTES),
        name=name,
    )
    return lambda *args: run(
        *[
            pltpu.with_memory_space_constraint(a, pltpu.VMEM if s is VMEM else pltpu.HBM) if s is not SMEM else a
            for a, s in zip(args, specs)
        ]
    )


def unit_rows(matrix):
    values = matrix.astype(jnp.float32)
    length = jnp.sqrt(jnp.sum(values * values, axis=1, keepdims=True) + epsilon)
    return (values / length, length)


def rows_kernel(core, image, text, first, other, raw_first, raw_other, sems):

    @pl.when(core[0] == 0)
    def _():
        pltpu.make_async_copy(image, raw_first, sems.at[0]).start()
        pltpu.make_async_copy(text, raw_other, sems.at[1]).start()

    @pl.when(core[0] != 0)
    def _():
        pltpu.make_async_copy(text, raw_first, sems.at[0]).start()
        pltpu.make_async_copy(image, raw_other, sems.at[1]).start()

    pltpu.make_async_copy(image, raw_first, sems.at[0]).wait()
    first[...] = unit_rows(raw_first[...])[0].astype(jnp.bfloat16)
    pltpu.make_async_copy(text, raw_other, sems.at[1]).wait()
    other[...] = unit_rows(raw_other[...])[0].astype(jnp.bfloat16)


def consts_kernel(numbers, after, after_too, consts):
    scale = jnp.exp(numbers[0:8])
    consts[0:8] = scale
    consts[8:16] = scale * (-math.log2(math.e))
    consts[16:24] = numbers[8:16] * (-math.log2(math.e))
    consts[24:32] = numbers[16:24] / (2 * after.shape[0] * SIDE * SIDE)


def negative(cosine, consts):
    power = cosine * consts[8:9, 0:1] + consts[16:17, 0:1]
    return (consts[24:25, 0:1] / (1.0 + jnp.exp2(power))).astype(jnp.bfloat16)


def positive(cosine, consts):
    power = cosine * consts[8:9, 0:1] + consts[16:17, 0:1]
    return (-consts[24:25, 0:1] / (1.0 + jnp.exp2(-power))).astype(jnp.bfloat16)


def joined(up, down):
    return jnp.concatenate([up[...], down[...]], 0)


def share(consts, left, *rights):
    right = jnp.concatenate([r[...] for r in rights], 0)
    return dot(negative(dot_t(left, right), consts), right)


def near_kernel(consts, back_first, back_second, ahead_first, ahead_second, other, other_second, near_first,
                near_second, part_back, part_ahead):
    rows = back_first.shape[0]
    left = jnp.concatenate([back_first[...], back_second[...], ahead_first[...], ahead_second[...]], 0)
    total = share(consts, left, other, other_second, near_first, near_second)
    part_back[...] = total[: 2 * rows]
    part_ahead[...] = total[2 * rows :]


def far_near_kernel(consts, far_first, far_second, other, other_second, near_first, near_second, late_others, part):
    part[...] = share(consts, joined(far_first, far_second), other, other_second, near_first, near_second, late_others)


def far_kernel(consts, part, far_first, far_second, far_others_first, far_others_second, share_first, share_second):
    rows = far_first.shape[0]
    left = joined(far_first, far_second)
    rights = (far_others_first[...], far_others_second[...])
    weights = [negative(dot_t(left, right), consts) for right in rights]
    total = part[...] + dot(weights[0], rights[0]) + dot(weights[1], rights[1])
    share_first[...] = total[:rows].astype(jnp.bfloat16)
    share_second[...] = total[rows:].astype(jnp.bfloat16)


def rest_kernel(consts, part_back, part_ahead, back_first, back_second, ahead_first, ahead_second, late_others,
                far_others_first, far_others_second, after, keep_back_first, share_back_second, share_ahead_first,
                keep_ahead_second):
    rows = back_first.shape[0]
    late = late_others[...]
    far_others = joined(far_others_first, far_others_second)
    left = jnp.concatenate([back_first[...], back_second[...], ahead_first[...], ahead_second[...]], 0)
    total = dot(negative(dot_t(left, late), consts), late)
    total += dot(negative(dot_t(left, far_others), consts), far_others)
    keep_back_first[...] = total[:rows] + part_back[:rows]
    share_back_second[...] = (total[rows : 2 * rows] + part_back[rows:]).astype(jnp.bfloat16)
    share_ahead_first[...] = (total[2 * rows : 3 * rows] + part_ahead[:rows]).astype(jnp.bfloat16)
    keep_ahead_second[...] = total[3 * rows :] + part_ahead[rows:]


def units_kernel(raw, after, unit, length):
    unit[...], length[...] = unit_rows(raw[...])


def own_kernel(consts, first, second, back_first, back_second, ahead_first, ahead_second, far_first, far_second, other,
               other_second, near_first, near_second, late_others, far_others_first, far_others_second, after, raw_other, own,
               their, unit_their, length_their):
    unit_their[...], length_their[...] = unit_rows(raw_other[...])
    for left, pairs, rights, out in (
        (first, joined(other, other_second),
         [joined(near_first, near_second), late_others[...], joined(far_others_first, far_others_second)], own),
        (other, joined(first, second),
         [joined(back_first, back_second), joined(ahead_first, ahead_second), joined(far_first, far_second)], their),
    ):
        cosine = dot_t(left[...], pairs)
        i = lax.broadcasted_iota(jnp.int32, cosine.shape, 0)
        j = lax.broadcasted_iota(jnp.int32, cosine.shape, 1)
        weights = jnp.where(i == j, positive(cosine, consts), negative(cosine, consts))
        total = dot(weights, pairs)
        for right in rights:
            total += dot(negative(dot_t(left[...], right), consts), right)
        out[...] = total


def relay_kernel(mine, got, out):
    out[...] = (mine[...] + got[...].astype(jnp.float32)).astype(jnp.bfloat16)


def last_kernel(core, consts, unit_own, length_own, unit_their, length_their, own, own_one, own_two, their, their_one,
                their_two, image_out, text_out, grads, sems):
    scale = consts[0:1, 0:1]
    for place, unit, length, mine, one, two in (
        (core[0], unit_own, length_own, own, own_one, own_two),
        (1 - core[0], unit_their, length_their, their, their_one, their_two),
    ):
        direction = scale * (mine[...] + one[...].astype(jnp.float32) + two[...].astype(jnp.float32))
        along = jnp.sum(unit[...] * direction, axis=1, keepdims=True)
        grads[place] = (direction - unit[...] * along) * (1.0 / length[...])
    copies = [pltpu.make_async_copy(grads.at[i], out, sems.at[i]) for i, out in enumerate((image_out, text_out))]
    for copy in copies:
        copy.start()
    for copy in copies:
        copy.wait()


def gate_kernel(value, after, out):
    pass


def gate(value, after):
    return pl.pallas_call(
        gate_kernel,
        out_shape=pltpu.VMEM(value.shape, value.dtype),
        in_specs=[VMEM, VMEM],
        out_specs=VMEM,
        input_output_aliases={0: 0},
        cost_estimate=pl.CostEstimate(flops=1, bytes_accessed=1, transcendentals=0),
        compiler_params=pltpu.CompilerParams(vmem_limit_bytes=VMEM_BYTES),
        name="gate",
    )(pltpu.with_memory_space_constraint(value, pltpu.VMEM), pltpu.with_memory_space_constraint(after, pltpu.VMEM))


def body(image_embed, text_embed, scale_logarithm, logit_bias, loss_grad):
    rows, width = image_embed.shape
    half = jax.ShapeDtypeStruct((rows, width), jnp.bfloat16)
    full = jax.ShapeDtypeStruct((rows, width), jnp.float32)
    double = jax.ShapeDtypeStruct((2 * rows, width), jnp.float32)
    core = (lax.axis_index("grp") % 2).astype(jnp.int32).reshape(1)
    numbers = jnp.concatenate(
        [jnp.broadcast_to(value, (8, 128)) for value in (scale_logarithm, logit_bias, loss_grad)], 0
    )
    unit = 2 * rows * rows * width

    first, other, raw_first, raw_other = call(
        rows_kernel,
        [half, half, half, half],
        [SMEM, HBM, HBM],
        10**8,
        "rows",
        scratch=[pltpu.SemaphoreType.DMA((2,))],
    )(core, image_embed, text_embed)

    back_first = hop(first, 1)
    ahead_second = cross(other, -1)
    other_second = swap(first)
    second = swap(other)
    (consts,) = call(consts_kernel, [jax.ShapeDtypeStruct((32, 128), jnp.float32)], [VMEM] * 3, 1, "consts")(
        numbers, second, other_second
    )
    back_second = hop(second, 1)
    ahead_first = cross(other_second, -1)
    back_first = gate(back_first, consts)
    ahead_second = gate(ahead_second, consts)
    far_first = hop(back_first, 1)
    far_second = hop(ahead_second, -1)
    near_others = (swap(back_first), swap(ahead_second))
    backs = (back_first, back_second)
    aheads = (ahead_first, ahead_second)
    late_others = swap(jnp.concatenate([back_second, ahead_first], 0))
    part_back, part_ahead = call(near_kernel, [double] * 2, [VMEM] * 9, 1, "near")(
        consts, *backs, *aheads, other, other_second, *near_others
    )
    column = jax.ShapeDtypeStruct((rows, 1), jnp.float32)
    unit_own, length_own = call(units_kernel, [full, column], [VMEM] * 2, 1, "units")(raw_first, part_back)
    far_first = gate(far_first, part_back)
    far_second = gate(far_second, unit_own)
    far_others_first = swap(far_first)
    far_others_second = swap(far_second)
    (part_far,) = call(far_near_kernel, [double], [VMEM] * 8, 1, "far_near")(
        consts, far_first, far_second, other, other_second, *near_others, late_others
    )
    share_first, share_second = call(far_kernel, [half, half], [VMEM] * 6, 8 * unit, "far")(
        consts, part_far, far_first, far_second, far_others_first, far_others_second
    )

    relay_first = hop(share_first, -1)
    relay_second = hop(share_second, 1)
    far_others = (far_others_first, far_others_second)
    keep_back_first, share_back_second, share_ahead_first, keep_ahead_second = call(
        rest_kernel, [full, half, half, full], [VMEM] * 11, C1, "rest"
    )(consts, part_back, part_ahead, *backs, *aheads, late_others, *far_others, share_first)
    their_one = cross_back(share_back_second, -1)
    own_one = hop(share_ahead_first, 1)
    (send_first,) = call(relay_kernel, [half], [VMEM] * 2, C3, "relay")(keep_back_first, relay_first)
    (send_second,) = call(relay_kernel, [half], [VMEM] * 2, C3, "relay")(keep_ahead_second, relay_second)
    own_two = hop(send_first, -1)
    their_two = cross_back(send_second, 1)
    own, their, unit_their, length_their = call(
        own_kernel, [full, full, full, column], [VMEM] * 18, C2, "own"
    )(
        consts, first, second, *backs, *aheads, far_first, far_second, other, other_second, *near_others, late_others,
        *far_others, send_first, raw_other,
    )
    image_gradient, text_gradient = call(
        last_kernel,
        [full, full],
        [SMEM] + [VMEM] * 11,
        C4,
        "last",
        out_specs=[HBM] * 2,
        scratch=[
            pltpu.VMEM((2, rows, width), jnp.float32),
            pltpu.SemaphoreType.DMA((2,)),
        ],
    )(core, consts, unit_own, length_own, unit_their, length_their, own, own_one, own_two, their, their_one, their_two)
    return (image_gradient, text_gradient)


def solution(mesh):
    placed = (P(AXES, None), P(AXES, None), P(), P(), P())
    return jax.shard_map(
        body,
        mesh=mesh,
        in_specs=placed,
        out_specs=(P(AXES, None), P(AXES, None)),
        check_vma=False,
    )
```

```python
import math

import jax
import jax.numpy as jnp
from jax import lax
from jax.experimental import pallas as pl
from jax.experimental.pallas import tpu as pltpu
from jax.sharding import PartitionSpec as P

epsilon = 1e-06
AXES = ("grp", "ing")
SIDE = 4
C1 = 1
C2 = 1
C3 = 1
C4 = 1
VMEM_BYTES = 16 * 1024 * 1024
VMEM = pl.BlockSpec(memory_space=pltpu.VMEM)
SMEM = pl.BlockSpec(memory_space=pltpu.SMEM)
HBM = pl.BlockSpec(memory_space=pl.ANY)


def moved(value, step, core_change=0, ring_change=0):
    size = SIDE * SIDE
    pairs = []
    for grp in range(lax.axis_size("grp")):
        target = grp ^ core_change
        for ing in range(size):
            y, x = divmod(ing, SIDE)
            if (grp ^ ring_change) % 2:
                y = (y + step) % SIDE
            else:
                x = (x + step) % SIDE
            pairs.append((grp * size + ing, target * size + y * SIDE + x))
    return lax.ppermute(value, AXES, pairs)


def hop(value, step):
    return moved(value, step)


def cross(value, step):
    return moved(value, step, 1, 1)


def cross_back(value, step):
    return moved(value, step, 1, 0)


def swap(value):
    return moved(value, 0, 1)


def dot_t(left, right):
    return lax.dot_general(left, right, (((1,), (1,)), ((), ())), preferred_element_type=jnp.float32)


def dot(left, right):
    return jnp.dot(left, right, preferred_element_type=jnp.float32)


def call(kernel, outs, specs, flops, name, out_specs=None, scratch=()):
    out_specs = out_specs or [VMEM] * len(outs)
    run = pl.pallas_call(
        kernel,
        out_shape=[pltpu.VMEM(o.shape, o.dtype) if s is VMEM else o for o, s in zip(outs, out_specs)],
        in_specs=specs,
        out_specs=out_specs,
        scratch_shapes=scratch,
        cost_estimate=pl.CostEstimate(flops=flops, bytes_accessed=1, transcendentals=0),
        compiler_params=pltpu.CompilerParams(vmem_limit_bytes=VMEM_BYTES),
        name=name,
    )
    return lambda *args: run(
        *[
            pltpu.with_memory_space_constraint(a, pltpu.VMEM if s is VMEM else pltpu.HBM) if s is not SMEM else a
            for a, s in zip(args, specs)
        ]
    )


def unit_rows(matrix):
    values = matrix.astype(jnp.float32)
    length = jnp.sqrt(jnp.sum(values * values, axis=1, keepdims=True) + epsilon)
    return (values / length, length)


def rows_kernel(core, image, text, first, other, both, raw_first, raw_other, sems):

    @pl.when(core[0] == 0)
    def _():
        pltpu.make_async_copy(image, raw_first, sems.at[0]).start()
        pltpu.make_async_copy(text, raw_other, sems.at[1]).start()

    @pl.when(core[0] != 0)
    def _():
        pltpu.make_async_copy(text, raw_first, sems.at[0]).start()
        pltpu.make_async_copy(image, raw_other, sems.at[1]).start()

    pltpu.make_async_copy(image, raw_first, sems.at[0]).wait()
    first[...] = unit_rows(raw_first[...])[0].astype(jnp.bfloat16)
    both[: first.shape[0]] = first[...]
    pltpu.make_async_copy(text, raw_other, sems.at[1]).wait()
    other[...] = unit_rows(raw_other[...])[0].astype(jnp.bfloat16)
    both[first.shape[0] :] = other[...]


def halves_kernel(both, up, down):
    rows = up.shape[0]
    up[...] = both[:rows]
    down[...] = both[rows:]


def consts_kernel(numbers, after, after_too, consts):
    scale = jnp.exp(numbers[0:8])
    consts[0:8] = scale
    consts[8:16] = scale * (-math.log2(math.e))
    consts[16:24] = numbers[8:16] * (-math.log2(math.e))
    consts[24:32] = numbers[16:24] / (2 * after.shape[0] * SIDE * SIDE)


def negative(cosine, consts):
    power = cosine * consts[8:9, 0:1] + consts[16:17, 0:1]
    return (consts[24:25, 0:1] / (1.0 + jnp.exp2(power))).astype(jnp.bfloat16)


def positive(cosine, consts):
    power = cosine * consts[8:9, 0:1] + consts[16:17, 0:1]
    return (-consts[24:25, 0:1] / (1.0 + jnp.exp2(-power))).astype(jnp.bfloat16)


def joined(up, down):
    return jnp.concatenate([up[...], down[...]], 0)


def share(consts, left, *rights):
    right = jnp.concatenate([r[...] for r in rights], 0)
    return dot(negative(dot_t(left, right), consts), right)


def near_kernel(consts, back_first, back_second, ahead_first, ahead_second, other, other_second, near_first,
                near_second, part_back, part_ahead):
    rows = back_first.shape[0]
    left = jnp.concatenate([back_first[...], back_second[...], ahead_first[...], ahead_second[...]], 0)
    total = share(consts, left, other, other_second, near_first, near_second)
    part_back[...] = total[: 2 * rows]
    part_ahead[...] = total[2 * rows :]


def far_near_kernel(consts, far_first, far_second, other, other_second, near_first, near_second, late_others, part):
    part[...] = share(consts, joined(far_first, far_second), other, other_second, near_first, near_second, late_others)


def far_kernel(consts, part, far_first, far_second, far_others_first, far_others_second, share_first, share_second):
    rows = far_first.shape[0]
    left = joined(far_first, far_second)
    rights = (far_others_first[...], far_others_second[...])
    weights = [negative(dot_t(left, right), consts) for right in rights]
    total = part[...] + dot(weights[0], rights[0]) + dot(weights[1], rights[1])
    share_first[...] = total[:rows].astype(jnp.bfloat16)
    share_second[...] = total[rows:].astype(jnp.bfloat16)


def rest_kernel(consts, part_back, part_ahead, back_first, back_second, ahead_first, ahead_second, late_others,
                far_others_first, far_others_second, after, keep_back_first, share_back_second, share_ahead_first,
                keep_ahead_second):
    rows = back_first.shape[0]
    late = late_others[...]
    far_others = joined(far_others_first, far_others_second)
    left = jnp.concatenate([back_first[...], back_second[...], ahead_first[...], ahead_second[...]], 0)
    total = dot(negative(dot_t(left, late), consts), late)
    total += dot(negative(dot_t(left, far_others), consts), far_others)
    keep_back_first[...] = total[:rows] + part_back[:rows]
    share_back_second[...] = (total[rows : 2 * rows] + part_back[rows:]).astype(jnp.bfloat16)
    share_ahead_first[...] = (total[2 * rows : 3 * rows] + part_ahead[:rows]).astype(jnp.bfloat16)
    keep_ahead_second[...] = total[3 * rows :] + part_ahead[rows:]


def units_kernel(raw, after, unit, length):
    unit[...], length[...] = unit_rows(raw[...])


def own_kernel(consts, first, second, back_first, back_second, ahead_first, ahead_second, far_first, far_second, other,
               other_second, near_first, near_second, late_others, far_others_first, far_others_second, after, raw_other, own,
               their, unit_their, length_their):
    unit_their[...], length_their[...] = unit_rows(raw_other[...])
    for left, pairs, rights, out in (
        (first, joined(other, other_second),
         [joined(near_first, near_second), late_others[...], joined(far_others_first, far_others_second)], own),
        (other, joined(first, second),
         [joined(back_first, back_second), joined(ahead_first, ahead_second), joined(far_first, far_second)], their),
    ):
        cosine = dot_t(left[...], pairs)
        i = lax.broadcasted_iota(jnp.int32, cosine.shape, 0)
        j = lax.broadcasted_iota(jnp.int32, cosine.shape, 1)
        weights = jnp.where(i == j, positive(cosine, consts), negative(cosine, consts))
        total = dot(weights, pairs)
        for right in rights:
            total += dot(negative(dot_t(left[...], right), consts), right)
        out[...] = total


def relay_kernel(mine, got, out):
    out[...] = (mine[...] + got[...].astype(jnp.float32)).astype(jnp.bfloat16)


def last_kernel(core, consts, unit_own, length_own, unit_their, length_their, own, own_one, own_two, their, their_one,
                their_two, image_out, text_out, grads, sems):
    scale = consts[0:1, 0:1]
    for place, unit, length, mine, one, two in (
        (core[0], unit_own, length_own, own, own_one, own_two),
        (1 - core[0], unit_their, length_their, their, their_one, their_two),
    ):
        direction = scale * (mine[...] + one[...].astype(jnp.float32) + two[...].astype(jnp.float32))
        along = jnp.sum(unit[...] * direction, axis=1, keepdims=True)
        grads[place] = (direction - unit[...] * along) * (1.0 / length[...])
    copies = [pltpu.make_async_copy(grads.at[i], out, sems.at[i]) for i, out in enumerate((image_out, text_out))]
    for copy in copies:
        copy.start()
    for copy in copies:
        copy.wait()


def gate_kernel(value, after, out):
    pass


def gate(value, after):
    return pl.pallas_call(
        gate_kernel,
        out_shape=pltpu.VMEM(value.shape, value.dtype),
        in_specs=[VMEM, VMEM],
        out_specs=VMEM,
        input_output_aliases={0: 0},
        cost_estimate=pl.CostEstimate(flops=1, bytes_accessed=1, transcendentals=0),
        compiler_params=pltpu.CompilerParams(vmem_limit_bytes=VMEM_BYTES),
        name="gate",
    )(pltpu.with_memory_space_constraint(value, pltpu.VMEM), pltpu.with_memory_space_constraint(after, pltpu.VMEM))


def body(image_embed, text_embed, scale_logarithm, logit_bias, loss_grad):
    rows, width = image_embed.shape
    half = jax.ShapeDtypeStruct((rows, width), jnp.bfloat16)
    full = jax.ShapeDtypeStruct((rows, width), jnp.float32)
    double = jax.ShapeDtypeStruct((2 * rows, width), jnp.float32)
    pair = jax.ShapeDtypeStruct((2 * rows, width), jnp.bfloat16)
    core = (lax.axis_index("grp") % 2).astype(jnp.int32).reshape(1)
    numbers = jnp.concatenate(
        [jnp.broadcast_to(value, (8, 128)) for value in (scale_logarithm, logit_bias, loss_grad)], 0
    )
    unit = 2 * rows * rows * width

    first, other, both, raw_first, raw_other = call(
        rows_kernel,
        [half, half, pair, half, half],
        [SMEM, HBM, HBM],
        10**8,
        "rows",
        scratch=[pltpu.SemaphoreType.DMA((2,))],
    )(core, image_embed, text_embed)

    back_first = hop(first, 1)
    ahead_second = cross(other, -1)
    other_second, second = call(halves_kernel, [half, half], [VMEM], 1, "halves")(swap(both))
    (consts,) = call(consts_kernel, [jax.ShapeDtypeStruct((32, 128), jnp.float32)], [VMEM] * 3, 1, "consts")(
        numbers, second, other_second
    )
    back_second = hop(second, 1)
    ahead_first = cross(other_second, -1)
    back_first = gate(back_first, consts)
    ahead_second = gate(ahead_second, consts)
    far_first = hop(back_first, 1)
    far_second = hop(ahead_second, -1)
    near_others = (swap(back_first), swap(ahead_second))
    backs = (back_first, back_second)
    aheads = (ahead_first, ahead_second)
    late_others = swap(jnp.concatenate([back_second, ahead_first], 0))
    part_back, part_ahead = call(near_kernel, [double] * 2, [VMEM] * 9, 1, "near")(
        consts, *backs, *aheads, other, other_second, *near_others
    )
    column = jax.ShapeDtypeStruct((rows, 1), jnp.float32)
    unit_own, length_own = call(units_kernel, [full, column], [VMEM] * 2, 1, "units")(raw_first, part_back)
    far_first = gate(far_first, part_back)
    far_second = gate(far_second, unit_own)
    far_others_first = swap(far_first)
    far_others_second = swap(far_second)
    (part_far,) = call(far_near_kernel, [double], [VMEM] * 8, 1, "far_near")(
        consts, far_first, far_second, other, other_second, *near_others, late_others
    )
    share_first, share_second = call(far_kernel, [half, half], [VMEM] * 6, 8 * unit, "far")(
        consts, part_far, far_first, far_second, far_others_first, far_others_second
    )

    relay_first = hop(share_first, -1)
    relay_second = hop(share_second, 1)
    far_others = (far_others_first, far_others_second)
    keep_back_first, share_back_second, share_ahead_first, keep_ahead_second = call(
        rest_kernel, [full, half, half, full], [VMEM] * 11, C1, "rest"
    )(consts, part_back, part_ahead, *backs, *aheads, late_others, *far_others, share_first)
    their_one = cross_back(share_back_second, -1)
    own_one = hop(share_ahead_first, 1)
    (send_first,) = call(relay_kernel, [half], [VMEM] * 2, C3, "relay")(keep_back_first, relay_first)
    (send_second,) = call(relay_kernel, [half], [VMEM] * 2, C3, "relay")(keep_ahead_second, relay_second)
    own_two = hop(send_first, -1)
    their_two = cross_back(send_second, 1)
    own, their, unit_their, length_their = call(
        own_kernel, [full, full, full, column], [VMEM] * 18, C2, "own"
    )(
        consts, first, second, *backs, *aheads, far_first, far_second, other, other_second, *near_others, late_others,
        *far_others, send_first, raw_other,
    )
    image_gradient, text_gradient = call(
        last_kernel,
        [full, full],
        [SMEM] + [VMEM] * 11,
        C4,
        "last",
        out_specs=[HBM] * 2,
        scratch=[
            pltpu.VMEM((2, rows, width), jnp.float32),
            pltpu.SemaphoreType.DMA((2,)),
        ],
    )(core, consts, unit_own, length_own, unit_their, length_their, own, own_one, own_two, their, their_one, their_two)
    return (image_gradient, text_gradient)


def solution(mesh):
    placed = (P(AXES, None), P(AXES, None), P(), P(), P())
    return jax.shard_map(
        body,
        mesh=mesh,
        in_specs=placed,
        out_specs=(P(AXES, None), P(AXES, None)),
        check_vma=False,
    )
```

```python
import math

import jax
import jax.numpy as jnp
from jax import lax
from jax.experimental import pallas as pl
from jax.experimental.pallas import tpu as pltpu
from jax.sharding import PartitionSpec as P

epsilon = 1e-06
AXES = ("grp", "ing")
SIDE = 4
C1 = 1
C2 = 1
C3 = 1
C4 = 1
VMEM_BYTES = 16 * 1024 * 1024
VMEM = pl.BlockSpec(memory_space=pltpu.VMEM)
SMEM = pl.BlockSpec(memory_space=pltpu.SMEM)
HBM = pl.BlockSpec(memory_space=pl.ANY)


def moved(value, step, core_change=0, ring_change=0):
    size = SIDE * SIDE
    pairs = []
    for grp in range(lax.axis_size("grp")):
        target = grp ^ core_change
        for ing in range(size):
            y, x = divmod(ing, SIDE)
            if (grp ^ ring_change) % 2:
                y = (y + step) % SIDE
            else:
                x = (x + step) % SIDE
            pairs.append((grp * size + ing, target * size + y * SIDE + x))
    return lax.ppermute(value, AXES, pairs)


def hop(value, step):
    return moved(value, step)


def cross(value, step):
    return moved(value, step, 1, 1)


def cross_back(value, step):
    return moved(value, step, 1, 0)


def swap(value):
    return moved(value, 0, 1)


def dot_t(left, right):
    return lax.dot_general(left, right, (((1,), (1,)), ((), ())), preferred_element_type=jnp.float32)


def dot(left, right):
    return jnp.dot(left, right, preferred_element_type=jnp.float32)


def call(kernel, outs, specs, flops, name, out_specs=None, scratch=()):
    out_specs = out_specs or [VMEM] * len(outs)
    run = pl.pallas_call(
        kernel,
        out_shape=[pltpu.VMEM(o.shape, o.dtype) if s is VMEM else o for o, s in zip(outs, out_specs)],
        in_specs=specs,
        out_specs=out_specs,
        scratch_shapes=scratch,
        cost_estimate=pl.CostEstimate(flops=flops, bytes_accessed=1, transcendentals=0),
        compiler_params=pltpu.CompilerParams(vmem_limit_bytes=VMEM_BYTES),
        name=name,
    )
    return lambda *args: run(
        *[
            pltpu.with_memory_space_constraint(a, pltpu.VMEM if s is VMEM else pltpu.HBM) if s is not SMEM else a
            for a, s in zip(args, specs)
        ]
    )


def unit_rows(matrix):
    values = matrix.astype(jnp.float32)
    length = jnp.sqrt(jnp.sum(values * values, axis=1, keepdims=True) + epsilon)
    return (values / length, length)


def rows_kernel(core, image, text, first, other, both, raw_first, raw_other, sems):

    @pl.when(core[0] == 0)
    def _():
        pltpu.make_async_copy(image, raw_first, sems.at[0]).start()
        pltpu.make_async_copy(text, raw_other, sems.at[1]).start()

    @pl.when(core[0] != 0)
    def _():
        pltpu.make_async_copy(text, raw_first, sems.at[0]).start()
        pltpu.make_async_copy(image, raw_other, sems.at[1]).start()

    pltpu.make_async_copy(image, raw_first, sems.at[0]).wait()
    first[...] = unit_rows(raw_first[...])[0].astype(jnp.bfloat16)
    both[: first.shape[0]] = first[...]
    pltpu.make_async_copy(text, raw_other, sems.at[1]).wait()
    other[...] = unit_rows(raw_other[...])[0].astype(jnp.bfloat16)
    both[first.shape[0] :] = other[...]


def halves_kernel(both, up, down):
    rows = up.shape[0]
    up[...] = both[:rows]
    down[...] = both[rows:]


def consts_kernel(numbers, after, after_too, consts):
    scale = jnp.exp(numbers[0:8])
    consts[0:8] = scale
    consts[8:16] = scale * (-math.log2(math.e))
    consts[16:24] = numbers[8:16] * (-math.log2(math.e))
    consts[24:32] = numbers[16:24] / (2 * after.shape[0] * SIDE * SIDE)


def negative(cosine, consts):
    power = cosine * consts[8:9, 0:1] + consts[16:17, 0:1]
    return (consts[24:25, 0:1] / (1.0 + jnp.exp2(power))).astype(jnp.bfloat16)


def positive(cosine, consts):
    power = cosine * consts[8:9, 0:1] + consts[16:17, 0:1]
    return (-consts[24:25, 0:1] / (1.0 + jnp.exp2(-power))).astype(jnp.bfloat16)


def joined(up, down):
    return jnp.concatenate([up[...], down[...]], 0)


def share(consts, left, *rights):
    right = jnp.concatenate([r[...] for r in rights], 0)
    return dot(negative(dot_t(left, right), consts), right)


def near_kernel(consts, back_first, back_second, ahead_first, ahead_second, other, other_second, near_first,
                near_second, part_back, part_ahead):
    rows = back_first.shape[0]
    left = jnp.concatenate([back_first[...], back_second[...], ahead_first[...], ahead_second[...]], 0)
    total = share(consts, left, other, other_second, near_first, near_second)
    part_back[...] = total[: 2 * rows]
    part_ahead[...] = total[2 * rows :]


def far_near_kernel(consts, far_first, far_second, other, other_second, near_first, near_second, late_others, part):
    part[...] = share(consts, joined(far_first, far_second), other, other_second, near_first, near_second, late_others)


def far_kernel(consts, part, far_first, far_second, far_others_first, far_others_second, share_first, share_second):
    rows = far_first.shape[0]
    left = joined(far_first, far_second)
    rights = (far_others_first[...], far_others_second[...])
    weights = [negative(dot_t(left, right), consts) for right in rights]
    total = part[...] + dot(weights[0], rights[0]) + dot(weights[1], rights[1])
    share_first[...] = total[:rows].astype(jnp.bfloat16)
    share_second[...] = total[rows:].astype(jnp.bfloat16)


def rest_kernel(consts, part_back, part_ahead, back_first, back_second, ahead_first, ahead_second, late_others,
                far_others_first, far_others_second, after, keep_back_first, share_back_second, share_ahead_first,
                keep_ahead_second):
    rows = back_first.shape[0]
    late = late_others[...]
    far_others = joined(far_others_first, far_others_second)
    left = jnp.concatenate([back_first[...], back_second[...], ahead_first[...], ahead_second[...]], 0)
    total = dot(negative(dot_t(left, late), consts), late)
    total += dot(negative(dot_t(left, far_others), consts), far_others)
    keep_back_first[...] = total[:rows] + part_back[:rows]
    share_back_second[...] = (total[rows : 2 * rows] + part_back[rows:]).astype(jnp.bfloat16)
    share_ahead_first[...] = (total[2 * rows : 3 * rows] + part_ahead[:rows]).astype(jnp.bfloat16)
    keep_ahead_second[...] = total[3 * rows :] + part_ahead[rows:]


def units_kernel(raw, after, unit, length):
    unit[...], length[...] = unit_rows(raw[...])


def own_kernel(consts, first, second, back_first, back_second, ahead_first, ahead_second, far_first, far_second, other,
               other_second, near_first, near_second, late_others, far_others_first, far_others_second, after, raw_other, own,
               their, unit_their, length_their):
    unit_their[...], length_their[...] = unit_rows(raw_other[...])
    for left, pairs, rights, out in (
        (first, joined(other, other_second),
         [joined(near_first, near_second), late_others[...], joined(far_others_first, far_others_second)], own),
        (other, joined(first, second),
         [joined(back_first, back_second), joined(ahead_first, ahead_second), joined(far_first, far_second)], their),
    ):
        cosine = dot_t(left[...], pairs)
        i = lax.broadcasted_iota(jnp.int32, cosine.shape, 0)
        j = lax.broadcasted_iota(jnp.int32, cosine.shape, 1)
        weights = jnp.where(i == j, positive(cosine, consts), negative(cosine, consts))
        total = dot(weights, pairs)
        for right in rights:
            total += dot(negative(dot_t(left[...], right), consts), right)
        out[...] = total


def relay_kernel(mine, got, out):
    out[...] = (mine[...] + got[...].astype(jnp.float32)).astype(jnp.bfloat16)


def last_kernel(core, consts, unit_own, length_own, unit_their, length_their, own, own_one, own_two, their, their_one,
                their_two, image_out, text_out, grads, sems):
    scale = consts[0:1, 0:1]
    copies = [pltpu.make_async_copy(grads.at[i], out, sems.at[i]) for i, out in enumerate((image_out, text_out))]
    for kind, (unit, length, mine, one, two) in enumerate((
        (unit_their, length_their, their, their_one, their_two),
        (unit_own, length_own, own, own_one, own_two),
    )):
        place = 1 - core[0] if kind == 0 else core[0]
        direction = scale * (mine[...] + one[...].astype(jnp.float32) + two[...].astype(jnp.float32))
        along = jnp.sum(unit[...] * direction, axis=1, keepdims=True)
        grads[place] = (direction - unit[...] * along) * (1.0 / length[...])
        for i, copy in enumerate(copies):
            pl.when(place == i)(copy.start)
    for copy in copies:
        copy.wait()


def gate_kernel(value, after, out):
    pass


def gate(value, after):
    return pl.pallas_call(
        gate_kernel,
        out_shape=pltpu.VMEM(value.shape, value.dtype),
        in_specs=[VMEM, VMEM],
        out_specs=VMEM,
        input_output_aliases={0: 0},
        cost_estimate=pl.CostEstimate(flops=1, bytes_accessed=1, transcendentals=0),
        compiler_params=pltpu.CompilerParams(vmem_limit_bytes=VMEM_BYTES),
        name="gate",
    )(pltpu.with_memory_space_constraint(value, pltpu.VMEM), pltpu.with_memory_space_constraint(after, pltpu.VMEM))


def body(image_embed, text_embed, scale_logarithm, logit_bias, loss_grad):
    rows, width = image_embed.shape
    half = jax.ShapeDtypeStruct((rows, width), jnp.bfloat16)
    full = jax.ShapeDtypeStruct((rows, width), jnp.float32)
    double = jax.ShapeDtypeStruct((2 * rows, width), jnp.float32)
    pair = jax.ShapeDtypeStruct((2 * rows, width), jnp.bfloat16)
    core = (lax.axis_index("grp") % 2).astype(jnp.int32).reshape(1)
    numbers = jnp.concatenate(
        [jnp.broadcast_to(value, (8, 128)) for value in (scale_logarithm, logit_bias, loss_grad)], 0
    )
    unit = 2 * rows * rows * width

    first, other, both, raw_first, raw_other = call(
        rows_kernel,
        [half, half, pair, half, half],
        [SMEM, HBM, HBM],
        10**8,
        "rows",
        scratch=[pltpu.SemaphoreType.DMA((2,))],
    )(core, image_embed, text_embed)

    back_first = hop(first, 1)
    ahead_second = cross(other, -1)
    other_second, second = call(halves_kernel, [half, half], [VMEM], 1, "halves")(swap(both))
    (consts,) = call(consts_kernel, [jax.ShapeDtypeStruct((32, 128), jnp.float32)], [VMEM] * 3, 1, "consts")(
        numbers, second, other_second
    )
    back_second = hop(second, 1)
    ahead_first = cross(other_second, -1)
    back_first = gate(back_first, consts)
    ahead_second = gate(ahead_second, consts)
    far_first = hop(back_first, 1)
    far_second = hop(ahead_second, -1)
    near_others = (swap(back_first), swap(ahead_second))
    backs = (back_first, back_second)
    aheads = (ahead_first, ahead_second)
    late_others = swap(jnp.concatenate([back_second, ahead_first], 0))
    part_back, part_ahead = call(near_kernel, [double] * 2, [VMEM] * 9, 1, "near")(
        consts, *backs, *aheads, other, other_second, *near_others
    )
    column = jax.ShapeDtypeStruct((rows, 1), jnp.float32)
    unit_own, length_own = call(units_kernel, [full, column], [VMEM] * 2, 1, "units")(raw_first, part_back)
    far_first = gate(far_first, part_back)
    far_second = gate(far_second, unit_own)
    far_others_first = swap(far_first)
    far_others_second = swap(far_second)
    (part_far,) = call(far_near_kernel, [double], [VMEM] * 8, 1, "far_near")(
        consts, far_first, far_second, other, other_second, *near_others, late_others
    )
    share_first, share_second = call(far_kernel, [half, half], [VMEM] * 6, 8 * unit, "far")(
        consts, part_far, far_first, far_second, far_others_first, far_others_second
    )

    relay_first = hop(share_first, -1)
    relay_second = hop(share_second, 1)
    far_others = (far_others_first, far_others_second)
    keep_back_first, share_back_second, share_ahead_first, keep_ahead_second = call(
        rest_kernel, [full, half, half, full], [VMEM] * 11, C1, "rest"
    )(consts, part_back, part_ahead, *backs, *aheads, late_others, *far_others, share_first)
    their_one = cross_back(share_back_second, -1)
    own_one = hop(share_ahead_first, 1)
    (send_first,) = call(relay_kernel, [half], [VMEM] * 2, C3, "relay")(keep_back_first, relay_first)
    (send_second,) = call(relay_kernel, [half], [VMEM] * 2, C3, "relay")(keep_ahead_second, relay_second)
    own_two = hop(send_first, -1)
    their_two = cross_back(send_second, 1)
    own, their, unit_their, length_their = call(
        own_kernel, [full, full, full, column], [VMEM] * 18, C2, "own"
    )(
        consts, first, second, *backs, *aheads, far_first, far_second, other, other_second, *near_others, late_others,
        *far_others, send_first, raw_other,
    )
    image_gradient, text_gradient = call(
        last_kernel,
        [full, full],
        [SMEM] + [VMEM] * 11,
        C4,
        "last",
        out_specs=[HBM] * 2,
        scratch=[
            pltpu.VMEM((2, rows, width), jnp.float32),
            pltpu.SemaphoreType.DMA((2,)),
        ],
    )(core, consts, unit_own, length_own, unit_their, length_their, own, own_one, own_two, their, their_one, their_two)
    return (image_gradient, text_gradient)


def solution(mesh):
    placed = (P(AXES, None), P(AXES, None), P(), P(), P())
    return jax.shard_map(
        body,
        mesh=mesh,
        in_specs=placed,
        out_specs=(P(AXES, None), P(AXES, None)),
        check_vma=False,
    )
```

```python
import math

import jax
import jax.numpy as jnp
from jax import lax
from jax.experimental import pallas as pl
from jax.experimental.pallas import tpu as pltpu
from jax.sharding import PartitionSpec as P

epsilon = 1e-06
AXES = ("grp", "ing")
SIDE = 4
C1 = 1
C2 = 1
C3 = 1
C4 = 1
VMEM_BYTES = 16 * 1024 * 1024
VMEM = pl.BlockSpec(memory_space=pltpu.VMEM)
SMEM = pl.BlockSpec(memory_space=pltpu.SMEM)
HBM = pl.BlockSpec(memory_space=pl.ANY)


def moved(value, step, core_change=0, ring_change=0):
    size = SIDE * SIDE
    pairs = []
    for grp in range(lax.axis_size("grp")):
        target = grp ^ core_change
        for ing in range(size):
            y, x = divmod(ing, SIDE)
            if (grp ^ ring_change) % 2:
                y = (y + step) % SIDE
            else:
                x = (x + step) % SIDE
            pairs.append((grp * size + ing, target * size + y * SIDE + x))
    return lax.ppermute(value, AXES, pairs)


def hop(value, step):
    return moved(value, step)


def cross(value, step):
    return moved(value, step, 1, 1)


def cross_back(value, step):
    return moved(value, step, 1, 0)


def swap(value):
    return moved(value, 0, 1)


def dot_t(left, right):
    return lax.dot_general(left, right, (((1,), (1,)), ((), ())), preferred_element_type=jnp.float32)


def dot(left, right):
    return jnp.dot(left, right, preferred_element_type=jnp.float32)


def call(kernel, outs, specs, flops, name, out_specs=None, scratch=()):
    out_specs = out_specs or [VMEM] * len(outs)
    run = pl.pallas_call(
        kernel,
        out_shape=[pltpu.VMEM(o.shape, o.dtype) if s is VMEM else o for o, s in zip(outs, out_specs)],
        in_specs=specs,
        out_specs=out_specs,
        scratch_shapes=scratch,
        cost_estimate=pl.CostEstimate(flops=flops, bytes_accessed=1, transcendentals=0),
        compiler_params=pltpu.CompilerParams(vmem_limit_bytes=VMEM_BYTES),
        name=name,
    )
    return lambda *args: run(
        *[
            pltpu.with_memory_space_constraint(a, pltpu.VMEM if s is VMEM else pltpu.HBM) if s is not SMEM else a
            for a, s in zip(args, specs)
        ]
    )


def unit_rows(matrix):
    values = matrix.astype(jnp.float32)
    length = jnp.sqrt(jnp.sum(values * values, axis=1, keepdims=True) + epsilon)
    return (values * (1.0 / length), length)


def rows_kernel(core, image, text, first, other, both, raw_first, raw_other, sems):

    @pl.when(core[0] == 0)
    def _():
        pltpu.make_async_copy(image, raw_first, sems.at[0]).start()
        pltpu.make_async_copy(text, raw_other, sems.at[1]).start()

    @pl.when(core[0] != 0)
    def _():
        pltpu.make_async_copy(text, raw_first, sems.at[0]).start()
        pltpu.make_async_copy(image, raw_other, sems.at[1]).start()

    pltpu.make_async_copy(image, raw_first, sems.at[0]).wait()
    half = unit_rows(raw_first[...])[0].astype(jnp.bfloat16)
    first[...] = half
    both[: first.shape[0]] = half
    pltpu.make_async_copy(text, raw_other, sems.at[1]).wait()
    half = unit_rows(raw_other[...])[0].astype(jnp.bfloat16)
    other[...] = half
    both[first.shape[0] :] = half


def halves_kernel(both, up, down):
    rows = up.shape[0]
    up[...] = both[:rows]
    down[...] = both[rows:]


def consts_kernel(numbers, after, after_too, consts):
    scale = jnp.exp(numbers[0:8])
    consts[0:8] = scale
    consts[8:16] = scale * (-math.log2(math.e))
    consts[16:24] = numbers[8:16] * (-math.log2(math.e))
    consts[24:32] = numbers[16:24] / (2 * after.shape[0] * SIDE * SIDE)


def negative(cosine, consts):
    power = cosine * consts[8:9, 0:1] + consts[16:17, 0:1]
    return (consts[24:25, 0:1] / (1.0 + jnp.exp2(power))).astype(jnp.bfloat16)


def positive(cosine, consts):
    power = cosine * consts[8:9, 0:1] + consts[16:17, 0:1]
    return (-consts[24:25, 0:1] / (1.0 + jnp.exp2(-power))).astype(jnp.bfloat16)


def joined(up, down):
    return jnp.concatenate([up[...], down[...]], 0)


def share(consts, left, *rights):
    right = jnp.concatenate([r[...] for r in rights], 0)
    return dot(negative(dot_t(left, right), consts), right)


def near_kernel(consts, back_first, back_second, ahead_first, ahead_second, other, other_second, near_first,
                near_second, part_back, part_ahead):
    rows = back_first.shape[0]
    left = jnp.concatenate([back_first[...], back_second[...], ahead_first[...], ahead_second[...]], 0)
    total = share(consts, left, other, other_second, near_first, near_second)
    part_back[...] = total[: 2 * rows]
    part_ahead[...] = total[2 * rows :]


def far_near_kernel(consts, far_first, far_second, other, other_second, near_first, near_second, late_others, part):
    part[...] = share(consts, joined(far_first, far_second), other, other_second, near_first, near_second, late_others)


def far_kernel(consts, part, far_first, far_second, far_others_first, far_others_second, share_first, share_second):
    rows = far_first.shape[0]
    left = joined(far_first, far_second)
    rights = (far_others_first[...], far_others_second[...])
    weights = [negative(dot_t(left, right), consts) for right in rights]
    total = part[...] + dot(weights[0], rights[0]) + dot(weights[1], rights[1])
    share_first[...] = total[:rows].astype(jnp.bfloat16)
    share_second[...] = total[rows:].astype(jnp.bfloat16)


def rest_kernel(consts, part_back, part_ahead, back_first, back_second, ahead_first, ahead_second, late_others,
                far_others_first, far_others_second, after, keep_back_first, share_back_second, share_ahead_first,
                keep_ahead_second):
    rows = back_first.shape[0]
    late = late_others[...]
    far_others = joined(far_others_first, far_others_second)
    left = jnp.concatenate([back_first[...], back_second[...], ahead_first[...], ahead_second[...]], 0)
    total = dot(negative(dot_t(left, late), consts), late)
    total += dot(negative(dot_t(left, far_others), consts), far_others)
    keep_back_first[...] = total[:rows] + part_back[:rows]
    share_back_second[...] = (total[rows : 2 * rows] + part_back[rows:]).astype(jnp.bfloat16)
    share_ahead_first[...] = (total[2 * rows : 3 * rows] + part_ahead[:rows]).astype(jnp.bfloat16)
    keep_ahead_second[...] = total[3 * rows :] + part_ahead[rows:]


def units_kernel(raw, after, unit, length):
    unit[...], length[...] = unit_rows(raw[...])


def own_kernel(consts, first, second, back_first, back_second, ahead_first, ahead_second, far_first, far_second, other,
               other_second, near_first, near_second, late_others, far_others_first, far_others_second, after, raw_other, own,
               their, unit_their, length_their):
    unit_their[...], length_their[...] = unit_rows(raw_other[...])
    for left, pairs, rights, out in (
        (first, joined(other, other_second),
         [joined(near_first, near_second), late_others[...], joined(far_others_first, far_others_second)], own),
        (other, joined(first, second),
         [joined(back_first, back_second), joined(ahead_first, ahead_second), joined(far_first, far_second)], their),
    ):
        cosine = dot_t(left[...], pairs)
        i = lax.broadcasted_iota(jnp.int32, cosine.shape, 0)
        j = lax.broadcasted_iota(jnp.int32, cosine.shape, 1)
        weights = jnp.where(i == j, positive(cosine, consts), negative(cosine, consts))
        total = dot(weights, pairs)
        for right in rights:
            total += dot(negative(dot_t(left[...], right), consts), right)
        out[...] = total


def relay_kernel(mine, got, out):
    out[...] = (mine[...] + got[...].astype(jnp.float32)).astype(jnp.bfloat16)


def last_kernel(core, consts, unit_own, length_own, unit_their, length_their, own, own_one, own_two, their, their_one,
                their_two, image_out, text_out, grads, sems):
    scale = consts[0:1, 0:1]
    for place, unit, length, mine, one, two in (
        (core[0], unit_own, length_own, own, own_one, own_two),
        (1 - core[0], unit_their, length_their, their, their_one, their_two),
    ):
        direction = scale * (mine[...] + one[...].astype(jnp.float32) + two[...].astype(jnp.float32))
        along = jnp.sum(unit[...] * direction, axis=1, keepdims=True)
        grads[place] = (direction - unit[...] * along) * (1.0 / length[...])
    copies = [pltpu.make_async_copy(grads.at[i], out, sems.at[i]) for i, out in enumerate((image_out, text_out))]
    for copy in copies:
        copy.start()
    for copy in copies:
        copy.wait()


def gate_kernel(value, after, out):
    pass


def gate(value, after):
    return pl.pallas_call(
        gate_kernel,
        out_shape=pltpu.VMEM(value.shape, value.dtype),
        in_specs=[VMEM, VMEM],
        out_specs=VMEM,
        input_output_aliases={0: 0},
        cost_estimate=pl.CostEstimate(flops=1, bytes_accessed=1, transcendentals=0),
        compiler_params=pltpu.CompilerParams(vmem_limit_bytes=VMEM_BYTES),
        name="gate",
    )(pltpu.with_memory_space_constraint(value, pltpu.VMEM), pltpu.with_memory_space_constraint(after, pltpu.VMEM))


def body(image_embed, text_embed, scale_logarithm, logit_bias, loss_grad):
    rows, width = image_embed.shape
    half = jax.ShapeDtypeStruct((rows, width), jnp.bfloat16)
    full = jax.ShapeDtypeStruct((rows, width), jnp.float32)
    double = jax.ShapeDtypeStruct((2 * rows, width), jnp.float32)
    pair = jax.ShapeDtypeStruct((2 * rows, width), jnp.bfloat16)
    core = (lax.axis_index("grp") % 2).astype(jnp.int32).reshape(1)
    numbers = jnp.concatenate(
        [jnp.broadcast_to(value, (8, 128)) for value in (scale_logarithm, logit_bias, loss_grad)], 0
    )
    unit = 2 * rows * rows * width

    first, other, both, raw_first, raw_other = call(
        rows_kernel,
        [half, half, pair, half, half],
        [SMEM, HBM, HBM],
        10**8,
        "rows",
        scratch=[pltpu.SemaphoreType.DMA((2,))],
    )(core, image_embed, text_embed)

    back_first = hop(first, 1)
    ahead_second = cross(other, -1)
    other_second, second = call(halves_kernel, [half, half], [VMEM], 1, "halves")(swap(both))
    (consts,) = call(consts_kernel, [jax.ShapeDtypeStruct((32, 128), jnp.float32)], [VMEM] * 3, 1, "consts")(
        numbers, second, other_second
    )
    back_second = hop(second, 1)
    ahead_first = cross(other_second, -1)
    back_first = gate(back_first, consts)
    ahead_second = gate(ahead_second, consts)
    far_first = hop(back_first, 1)
    far_second = hop(ahead_second, -1)
    near_others = (swap(back_first), swap(ahead_second))
    backs = (back_first, back_second)
    aheads = (ahead_first, ahead_second)
    late_others = swap(jnp.concatenate([back_second, ahead_first], 0))
    part_back, part_ahead = call(near_kernel, [double] * 2, [VMEM] * 9, 1, "near")(
        consts, *backs, *aheads, other, other_second, *near_others
    )
    column = jax.ShapeDtypeStruct((rows, 1), jnp.float32)
    unit_own, length_own = call(units_kernel, [full, column], [VMEM] * 2, 1, "units")(raw_first, part_back)
    far_first = gate(far_first, part_back)
    far_second = gate(far_second, unit_own)
    far_others_first = swap(far_first)
    far_others_second = swap(far_second)
    (part_far,) = call(far_near_kernel, [double], [VMEM] * 8, 1, "far_near")(
        consts, far_first, far_second, other, other_second, *near_others, late_others
    )
    share_first, share_second = call(far_kernel, [half, half], [VMEM] * 6, 8 * unit, "far")(
        consts, part_far, far_first, far_second, far_others_first, far_others_second
    )

    relay_first = hop(share_first, -1)
    relay_second = hop(share_second, 1)
    far_others = (far_others_first, far_others_second)
    keep_back_first, share_back_second, share_ahead_first, keep_ahead_second = call(
        rest_kernel, [full, half, half, full], [VMEM] * 11, C1, "rest"
    )(consts, part_back, part_ahead, *backs, *aheads, late_others, *far_others, share_first)
    their_one = cross_back(share_back_second, -1)
    own_one = hop(share_ahead_first, 1)
    (send_first,) = call(relay_kernel, [half], [VMEM] * 2, C3, "relay")(keep_back_first, relay_first)
    (send_second,) = call(relay_kernel, [half], [VMEM] * 2, C3, "relay")(keep_ahead_second, relay_second)
    own_two = hop(send_first, -1)
    their_two = cross_back(send_second, 1)
    own, their, unit_their, length_their = call(
        own_kernel, [full, full, full, column], [VMEM] * 18, C2, "own"
    )(
        consts, first, second, *backs, *aheads, far_first, far_second, other, other_second, *near_others, late_others,
        *far_others, send_first, raw_other,
    )
    image_gradient, text_gradient = call(
        last_kernel,
        [full, full],
        [SMEM] + [VMEM] * 11,
        C4,
        "last",
        out_specs=[HBM] * 2,
        scratch=[
            pltpu.VMEM((2, rows, width), jnp.float32),
            pltpu.SemaphoreType.DMA((2,)),
        ],
    )(core, consts, unit_own, length_own, unit_their, length_their, own, own_one, own_two, their, their_one, their_two)
    return (image_gradient, text_gradient)


def solution(mesh):
    placed = (P(AXES, None), P(AXES, None), P(), P(), P())
    return jax.shard_map(
        body,
        mesh=mesh,
        in_specs=placed,
        out_specs=(P(AXES, None), P(AXES, None)),
        check_vma=False,
    )
```
